128 devices in a mesh: inp: 16 (over x, z), tim: 8 (over y, core).
Axes of the slice: x: 4, y: 4, z: 4, core: 2. Of those that a mesh axis runs over, the one named last changes fastest.
Arguments:
- voltages: int32 [2, 1024, 131072], P(None, 'inp', 'tim'), may hold values from -128 to 127
- scale_exps: int32 [1024, 32], P('inp', 'tim'), may hold values from 0 to 3
- owner_table: int32 [144], replicated, may hold values from 0 to 127, as said below
Outputs:
- visibilities: float32 [256, 1024, 1024], P(('inp', 'tim'))
The draws below stay inside these ranges and needn't reach their ends.
Inputs may be any that keep to these rules, and one draw needn't show every extreme that they name: owner_table[o] names the device whose index along inp, times the size of tim, plus its index along tim, is the value. No device owns more than 2 output channels, and some device owns exactly 2.
All inputs are finite; a program needn't handle non-finite values.
Results may differ from the reference program's by a relative error of at most 0.0035.
Values may be sent and summed in bfloat16 or wider, within the bound.
A program may use at most 192 MiB of HBM per device.

```python
import math
import jax
import jax.numpy as jnp
from jax import lax

F = 4096
AVG = 24
CH = 144
TAPS = 4
INPUTS = 1024
SPECTRA = 32
CAP = 2
SLOTS = 256


def draw_owner_table(key, part):
    key = jax.random.fold_in(key, 11)
    first, second, third = jax.random.split(key, 3)
    scores = jax.random.permutation(first, SLOTS).astype(jnp.int32)
    chosen_owner = jax.random.randint(second, (), 0, SLOTS // CAP)
    pool_owner = jnp.arange(SLOTS, dtype=jnp.int32) // CAP
    scores = jnp.where(pool_owner == chosen_owner, scores - SLOTS, scores)
    order = jnp.argsort(scores, stable=True)
    owners = (order[:CH] // CAP).astype(jnp.int32)
    shuffle = jax.random.permutation(third, CH)
    return owners[shuffle].astype(jnp.int32)


def with_ends(drawn, rng, smallest, high):
    extent = drawn.shape
    spot = [jax.random.randint(jax.random.fold_in(rng, axis), (), 0, extent[axis]) for axis in range(len(extent))]
    drawn = drawn.at[tuple(spot)].set(smallest)
    longest = extent.index(max(extent))
    spot[longest] = (spot[longest] + 1) % extent[longest]
    return drawn.at[tuple(spot)].set(high)


def setup_inputs(seed: int = 0) -> dict:
    arg_keys = jax.random.split(jax.random.key(seed), 4)
    return {
        "voltages": with_ends(jax.random.randint(arg_keys[0], (2, INPUTS, SPECTRA * F), -128, 128), jax.random.fold_in(arg_keys[0], 1), -128, 127).astype(jnp.int32),
        "scale_exps": with_ends(jax.random.randint(arg_keys[1], (INPUTS, SPECTRA), 0, 4), jax.random.fold_in(arg_keys[1], 1), 0, 3).astype(jnp.int32),
        "owner_table": draw_owner_table(jax.random.fold_in(arg_keys[3], 71), 0),
    }


def window_table():
    length = TAPS * F
    steps = jnp.arange(length, dtype=jnp.int32).astype(jnp.float32)
    centre = (steps + 0.5 - length / 2.0) / F
    taper = 0.5 - 0.5 * jnp.cos(2.0 * math.pi * (steps + 0.5) / length)
    return (jnp.sinc(centre) * taper).reshape(TAPS, F)

def owner_rows(owner_table, cap):
    index = jnp.arange(owner_table.shape[0], dtype=jnp.int32)
    same = owner_table[:, None] == owner_table[None, :]
    earlier = index[None, :] < index[:, None]
    slot = lax.optimization_barrier(jnp.sum((same & earlier).astype(jnp.int32), axis=1))
    return (owner_table * cap + slot).astype(jnp.int32)

def reference(voltages, scale_exps, owner_table):
    inputs = voltages.shape[1]
    spectra = scale_exps.shape[1]
    scale = jnp.exp2(scale_exps.astype(jnp.float32)) / 128.0
    samples = (voltages.reshape(2, inputs, spectra, F).astype(jnp.float32) * scale[None, :, :, None]).astype(jnp.bfloat16)
    padded = jnp.concatenate([jnp.zeros((2, inputs, TAPS - 1, F), jnp.bfloat16), samples], axis=2)
    weights = window_table()
    filtered = jnp.zeros((2, inputs, spectra, F), jnp.float32)
    for tap in range(TAPS):
        filtered = filtered + weights[tap][None, None, None, :] * padded[:, :, tap:tap + spectra, :].astype(jnp.float32)
    filtered = filtered.astype(jnp.bfloat16)
    signal = filtered[0].astype(jnp.float32) + 1j * filtered[1].astype(jnp.float32)
    spectrum = jnp.fft.fft(signal, axis=-1) / math.sqrt(F)
    real_all = jnp.real(spectrum).astype(jnp.bfloat16)
    imag_all = jnp.imag(spectrum).astype(jnp.bfloat16)
    upper = jnp.arange(inputs, dtype=jnp.int32)[:, None] <= jnp.arange(inputs, dtype=jnp.int32)[None, :]
    inverse = 1.0 / (spectra * AVG)
    offsets = jnp.arange(AVG, dtype=jnp.int32)

    def correlate(channel):
        bins = ((channel * AVG + offsets - AVG * CH // 2) % F).astype(jnp.int32)
        real_part = jnp.take(real_all, bins, axis=2).reshape(inputs, spectra * AVG).astype(jnp.float32)
        imag_part = jnp.take(imag_all, bins, axis=2).reshape(inputs, spectra * AVG).astype(jnp.float32)
        stacked = jnp.concatenate([real_part, imag_part], axis=1)
        swapped = jnp.concatenate([imag_part, -real_part], axis=1)
        real_gram = jnp.dot(stacked, stacked.T, precision=lax.Precision.HIGHEST)
        imag_gram = jnp.dot(swapped, stacked.T, precision=lax.Precision.HIGHEST)
        return jnp.where(upper, real_gram, imag_gram) * inverse
    every = lax.map(correlate, jnp.arange(CH, dtype=jnp.int32))
    rows = owner_rows(owner_table, CAP)
    result = jnp.zeros((SLOTS, inputs, inputs), jnp.float32)
    return result.at[rows].set(every)
```

```python
import functools
import math

import jax
import jax.numpy as jnp
import numpy as np
from jax import lax
from jax.experimental import pallas as pl
from jax.experimental.pallas import tpu as pltpu
from jax.sharding import PartitionSpec as P

F = 4096
AVG = 24
CH = 144
TAPS = 4
CAP = 2
R1 = 16
R2 = 256
LANES = 128


def window_table():
    length = TAPS * F
    steps = np.arange(length, dtype=np.float64)
    centre = (steps + 0.5 - length / 2.0) / F
    taper = 0.5 - 0.5 * np.cos(2.0 * math.pi * (steps + 0.5) / length)
    table = (np.sinc(centre) * taper).reshape(TAPS, 1, F)
    return np.broadcast_to(table, (TAPS, 8, F)).astype(np.float32)


def twist_table():
    phase = np.arange(R1)[:, None] * np.arange(R2)[None, :]
    angle = 2.0 * math.pi * phase / F
    table = np.stack([np.cos(angle), np.sin(angle)]) / math.sqrt(F)
    return np.broadcast_to(table[:, :, None, :], (2, R1, 8, R2)).astype(np.float32)


def radix_table():
    phase = np.arange(R2)[:, None] * np.arange(R2)[None, :] % R2
    angle = 2.0 * math.pi * phase / R2
    cosine, sine = np.cos(angle), np.sin(angle)
    table = np.concatenate(
        [np.concatenate([cosine, sine], axis=1), np.concatenate([-sine, cosine], axis=1)], axis=0
    )
    return table.astype(np.float32)


def owner_rows(owner_table, cap):
    index = jnp.arange(owner_table.shape[0], dtype=jnp.int32)
    same = owner_table[:, None] == owner_table[None, :]
    earlier = index[None, :] < index[:, None]
    slot = jnp.sum((same & earlier).astype(jnp.int32), axis=1)
    return owner_table * cap + slot


def four(a, b, c, d):
    sr, si = a[0] + c[0], a[1] + c[1]
    tr, ti = a[0] - c[0], a[1] - c[1]
    ur, ui = b[0] + d[0], b[1] + d[1]
    vr, vi = b[0] - d[0], b[1] - d[1]
    return (sr + ur, si + ui), (tr + vi, ti - vr), (sr - ur, si - ui), (tr - vi, ti + vr)


def turn(value, power):
    re, im = value
    power %= 16
    if power == 0:
        return value
    if power == 4:
        return im, -re
    root = math.sqrt(0.5)
    if power == 2:
        return (re + im) * root, (im - re) * root
    if power == 6:
        return (im - re) * root, (re + im) * (-root)
    cosine, sine = math.cos(2 * math.pi * power / 16), math.sin(2 * math.pi * power / 16)
    return re * cosine + im * sine, im * cosine - re * sine


def sixteen(x):
    inner = [four(x[b], x[4 + b], x[8 + b], x[12 + b]) for b in range(4)]
    out = [None] * 16
    for c in range(4):
        row = four(*[turn(inner[b][c], b * c) for b in range(4)])
        for d in range(4):
            out[c + 4 * d] = row[d]
    return out


def channel_kernel(first_ref, x0, x1, x2, x3, x4, window, twist, table, out, turned, spectrum):
    xs = (x0, x1, x2, x3, x4)
    step = pl.program_id(0)
    block = 16

    def columns(half, carry):
        base = half * LANES
        lanes2 = pl.ds(pl.multiple_of(base, LANES), LANES)
        for s in range(2):
            for r in range(2):
                series = []
                for n in range(R1):
                    lanes = pl.ds(pl.multiple_of(base + n * R2, LANES), LANES)
                    parts = []
                    for c in range(2):
                        total = None
                        for tap in range(TAPS):
                            value = xs[s + tap][c, :, lanes].astype(jnp.float32)[8 * r : 8 * r + 8]
                            term = window[tap, :, lanes] * value
                            total = term if total is None else total + term
                        parts.append(total.astype(jnp.bfloat16).astype(jnp.float32))
                    series.append(tuple(parts))
                result = sixteen(series)
                row = pl.multiple_of(step * block + s * 64 + 8 * r, 8)
                for m in range(R1):
                    re, im = result[m]
                    cosine, sine = twist[0, m, :, lanes2], twist[1, m, :, lanes2]
                    turned[m, pl.ds(row, 8), lanes2] = re * cosine + im * sine
                    turned[m, pl.ds(row, 8), pl.ds(pl.multiple_of(base + R2, LANES), LANES)] = (
                        im * cosine - re * sine
                    )
        return carry

    lax.fori_loop(0, R2 // LANES, columns, 0)

    @pl.when(step == pl.num_programs(0) - 1)
    def _():
        weights = table[...]
        for m in range(0, R1, 2):
            pair = turned[m : m + 2].reshape(2 * LANES, 2 * R2).astype(jnp.bfloat16)
            result = lax.dot_general(
                weights, pair, (((1,), (1,)), ((), ())), preferred_element_type=jnp.float32
            )
            for d in range(2):
                for e in range(2):
                    spectrum[d, pl.ds(m + e, R2, stride=R1), :] = result[
                        d * R2 : (d + 1) * R2, e * LANES : (e + 1) * LANES
                    ]

        def place(slot, carry):
            start = pl.multiple_of(first_ref[slot], 8)
            both = [spectrum[d, pl.ds(start, AVG), :] for d in range(2)]
            out[slot] = jnp.concatenate(both, axis=0).astype(jnp.bfloat16)
            return carry

        lax.fori_loop(0, out.shape[0], place, 0, unroll=4)


def channel_call(first, xs, window, twist, table):
    slots = first.shape[0]
    block = 16
    steps = xs[0].shape[1] // block
    spec = pl.BlockSpec((2, block, F), lambda i, *_: (0, i, 0))
    whole = lambda shape: pl.BlockSpec(shape, lambda i, *_: (0,) * len(shape))
    return pl.pallas_call(
        channel_kernel,
        out_shape=jax.ShapeDtypeStruct((slots, 2 * AVG, LANES), jnp.bfloat16),
        grid_spec=pltpu.PrefetchScalarGridSpec(
            num_scalar_prefetch=1,
            grid=(steps,),
            in_specs=[spec] * 5 + [whole(window.shape), whole(twist.shape), whole(table.shape)],
            out_specs=whole((slots, 2 * AVG, LANES)),
            scratch_shapes=[
                pltpu.VMEM((R1, LANES, 2 * R2), jnp.float32),
                pltpu.VMEM((2, F, LANES), jnp.float32),
            ],
        ),
        compiler_params=pltpu.CompilerParams(vmem_limit_bytes=48 * 2**20),
        cost_estimate=pl.CostEstimate(flops=2 * 10**9, bytes_accessed=9 * 2**20, transcendentals=0),
        name="channels",
    )(first, *xs, window, twist, table)


def correlate_kernel(n_inp, n_tim, valid_ref, *refs):
    chunks = len(refs) - 3
    pieces, out, rows_k, rows_i = refs[:chunks], refs[chunks], refs[chunks + 1], refs[chunks + 2]
    slot = pl.program_id(0)
    width = out.shape[1]
    depth = rows_k.shape[1]
    inverse = 1.0 / depth

    @pl.when(valid_ref[slot] == 0)
    def _():
        out[...] = jnp.zeros_like(out)

    @pl.when(valid_ref[slot] != 0)
    def _():
        low = lax.broadcasted_iota(jnp.int32, (2 * AVG, LANES), 1) < LANES // 2

        def arrange(q, carry):
            lanes = pl.ds(pl.multiple_of(q * LANES, LANES), LANES)
            for chunk in range(chunks):
                for u in range(n_tim // 2):
                    group = [
                        [
                            pieces[chunk][(2 * q + e) * n_tim + 2 * u + v, 0].astype(jnp.float32)
                            for v in range(2)
                        ]
                        for e in range(2)
                    ]
                    for c in range(2):
                        even, odd = [
                            jnp.concatenate([group[e][v][AVG * c : AVG * c + AVG] for v in range(2)], axis=0)
                            for e in range(2)
                        ]
                        first = jnp.where(low, even, pltpu.roll(odd, LANES // 2, 1))
                        second = jnp.where(low, pltpu.roll(even, LANES // 2, 1), odd)
                        base = (chunk * (n_tim // 2) + u) * 4 * AVG
                        rows_k[c, base : base + 2 * AVG, lanes] = first.astype(jnp.bfloat16)
                        rows_k[c, base + 2 * AVG : base + 4 * AVG, lanes] = second.astype(jnp.bfloat16)
            for c in range(2):
                rows_i[c, lanes, :] = rows_k[c, :, lanes].T
            return carry

        lax.fori_loop(0, width // LANES, arrange, 0)
        tile = 256
        upper = lax.broadcasted_iota(jnp.int32, (tile, tile), 0) <= lax.broadcasted_iota(
            jnp.int32, (tile, tile), 1
        )

        def dot(a, b):
            return jnp.dot(a, b, preferred_element_type=jnp.float32)

        for i in range(width // tile):
            re_i, im_i = [rows_i[c, i * tile : (i + 1) * tile, :] for c in range(2)]
            for j in range(width // tile):
                re_j, im_j = [rows_k[c, :, j * tile : (j + 1) * tile] for c in range(2)]
                real = imag = None
                if i <= j:
                    real = dot(re_i, re_j) + dot(im_i, im_j)
                if i >= j:
                    imag = dot(im_i, re_j) - dot(re_i, im_j)
                value = real if imag is None else imag if real is None else jnp.where(upper, real, imag)
                out[0, i * tile : (i + 1) * tile, j * tile : (j + 1) * tile] = value * inverse


def correlate_call(n_inp, n_tim, valid, pieces):
    width = n_inp * LANES // 2
    depth = n_tim * len(pieces) * 2 * AVG
    pieces = [p.reshape(n_inp * n_tim, CAP, 2 * AVG, LANES) for p in pieces]
    return pl.pallas_call(
        functools.partial(correlate_kernel, n_inp, n_tim),
        out_shape=jax.ShapeDtypeStruct((CAP, width, width), jnp.float32),
        grid_spec=pltpu.PrefetchScalarGridSpec(
            num_scalar_prefetch=1,
            grid=(CAP,),
            in_specs=[pl.BlockSpec((n_inp * n_tim, 1, 2 * AVG, LANES), lambda s, *_: (0, s, 0, 0))]
            * len(pieces),
            out_specs=pl.BlockSpec((1, width, width), lambda s, *_: (s, 0, 0)),
            scratch_shapes=[
                pltpu.VMEM((2, depth, width), jnp.bfloat16),
                pltpu.VMEM((2, width, depth), jnp.bfloat16),
            ],
        ),
        compiler_params=pltpu.CompilerParams(vmem_limit_bytes=48 * 2**20),
        cost_estimate=pl.CostEstimate(flops=10**10, bytes_accessed=15 * 2**20, transcendentals=0),
        name="correlate",
    )(valid, *pieces)


def body(voltages, scale_exps, owner_table):
    n_inp = lax.axis_size("inp")
    n_tim = lax.axis_size("tim")
    devices = n_inp * n_tim
    spec_dev = voltages.shape[2] // F
    scale = jnp.exp2(scale_exps.astype(jnp.float32)) / 128.0
    own = [
        (voltages[:, :, s * F : (s + 1) * F].astype(jnp.float32) * scale[None, :, s : s + 1]).astype(
            jnp.bfloat16
        )
        for s in range(spec_dev)
    ]
    ahead = [(source, source + 1) for source in range(n_tim - 1)]
    before = {s: lax.ppermute(own[s], "tim", ahead) for s in (3, 2, 1)}

    rows = owner_rows(owner_table, CAP)
    match = rows[None, :] == jnp.arange(devices * CAP, dtype=jnp.int32)[:, None]
    valid = jnp.any(match, axis=1).astype(jnp.int32)
    which = jnp.sum(jnp.where(match, jnp.arange(CH, dtype=jnp.int32)[None, :], 0), axis=1)
    first = (which * AVG - AVG * CH // 2) % F
    me = lax.axis_index("inp") * n_tim + lax.axis_index("tim")
    mine = lax.dynamic_slice(valid, (me * CAP,), (CAP,))

    window = jnp.asarray(window_table())
    twist = jnp.asarray(twist_table())
    table = jnp.asarray(radix_table()).astype(jnp.bfloat16)

    late = channel_call(first, (before[3], own[0], own[1], own[2], own[3]), window, twist, table)
    late = lax.all_to_all(late, ("inp", "tim"), split_axis=0, concat_axis=0, tiled=True)
    early = channel_call(first, (before[1], before[2], before[3], own[0], own[1]), window, twist, table)
    early = lax.all_to_all(early, ("inp", "tim"), split_axis=0, concat_axis=0, tiled=True)
    return correlate_call(n_inp, n_tim, mine, [late, early])


def solution(mesh):
    return jax.shard_map(
        body,
        mesh=mesh,
        in_specs=(P(None, "inp", "tim"), P("inp", "tim"), P()),
        out_specs=P(("inp", "tim"), None, None),
        check_vma=False,
    )
```

```python
import functools
import math

import jax
import jax.numpy as jnp
import numpy as np
from jax import lax
from jax.experimental import pallas as pl
from jax.experimental.pallas import tpu as pltpu
from jax.sharding import PartitionSpec as P

F = 4096
AVG = 24
CH = 144
TAPS = 4
CAP = 2
R1 = 16
R2 = 256
LANES = 128
VMEM = 60 * 2**20
MIXED = 16


def window_table():
    length = TAPS * F
    steps = np.arange(length, dtype=np.float64)
    centre = (steps + 0.5 - length / 2.0) / F
    taper = 0.5 - 0.5 * np.cos(2.0 * math.pi * (steps + 0.5) / length)
    table = (np.sinc(centre) * taper).reshape(TAPS, 1, F)
    table = np.concatenate([table, np.zeros((1, 1, F))], axis=0)
    return np.broadcast_to(table, (TAPS + 1, 8, F)).astype(np.float32)


def twist_table():
    phase = np.arange(R1)[:, None] * np.arange(R2)[None, :]
    angle = 2.0 * math.pi * phase / F
    table = np.stack([np.cos(angle), np.sin(angle)]) / math.sqrt(F)
    return np.broadcast_to(table[:, :, None, :], (2, R1, 8, R2)).astype(np.float32)


def radix_table():
    phase = np.arange(R2)[:, None] * np.arange(R2)[None, :] % R2
    angle = 2.0 * math.pi * phase / R2
    cosine, sine = np.cos(angle), np.sin(angle)
    table = np.concatenate(
        [np.concatenate([cosine, sine], axis=1), np.concatenate([-sine, cosine], axis=1)], axis=0
    )
    return table.astype(np.float32)


def owner_rows(owner_table, cap):
    index = jnp.arange(owner_table.shape[0], dtype=jnp.int32)
    same = owner_table[:, None] == owner_table[None, :]
    earlier = index[None, :] < index[:, None]
    slot = jnp.sum((same & earlier).astype(jnp.int32), axis=1)
    return owner_table * cap + slot


def four(a, b, c, d):
    sr, si = a[0] + c[0], a[1] + c[1]
    tr, ti = a[0] - c[0], a[1] - c[1]
    ur, ui = b[0] + d[0], b[1] + d[1]
    vr, vi = b[0] - d[0], b[1] - d[1]
    return (sr + ur, si + ui), (tr + vi, ti - vr), (sr - ur, si - ui), (tr - vi, ti + vr)


def turn(value, power):
    re, im = value
    power %= 16
    if power == 0:
        return value
    if power == 4:
        return im, -re
    root = math.sqrt(0.5)
    if power == 2:
        return (re + im) * root, (im - re) * root
    if power == 6:
        return (im - re) * root, (re + im) * (-root)
    cosine, sine = math.cos(2 * math.pi * power / 16), math.sin(2 * math.pi * power / 16)
    return re * cosine + im * sine, im * cosine - re * sine


def sixteen(x):
    inner = [four(x[b], x[4 + b], x[8 + b], x[12 + b]) for b in range(4)]
    out = [None] * 16
    for c in range(4):
        row = four(*[turn(inner[b][c], b * c) for b in range(4)])
        for d in range(4):
            out[c + 4 * d] = row[d]
    return out


def channel_kernel(plans, count, first_ref, *refs):
    xs, (window, twist, table) = refs[:count], refs[count : count + 3]
    prior, (out, turned, spectrum) = refs[count + 3 : -3], refs[-3:]
    step = pl.program_id(0)
    spectra = len(plans[0])
    block = xs[0].shape[1]
    inputs = turned.shape[1] // spectra
    slots = out.shape[0] * out.shape[1]
    wrapped = first_ref[slots] != 0

    def columns(plan, half):
        base = half * LANES
        lanes2 = pl.ds(pl.multiple_of(base, LANES), LANES)
        lanes3 = pl.ds(pl.multiple_of(base + R2, LANES), LANES)
        for s, (blocks, cut) in enumerate(plan):
            for r in range(block // 8):
                series = []
                for n in range(R1):
                    lanes = pl.ds(pl.multiple_of(base + n * R2, LANES), LANES)
                    parts = []
                    for c in range(2):
                        total = None
                        for tap in range(TAPS):
                            index, part = blocks[tap]
                            value = xs[index][part + c, :, lanes].astype(jnp.float32)[8 * r : 8 * r + 8]
                            which = tap if tap >= cut else jnp.where(wrapped, TAPS, tap)
                            term = window[which, :, lanes] * value
                            total = term if total is None else total + term
                        parts.append(total.astype(jnp.bfloat16).astype(jnp.float32))
                    series.append(tuple(parts))
                result = sixteen(series)
                row = pl.ds(pl.multiple_of(step * block + s * inputs + 8 * r, 8), 8)
                for m in range(R1):
                    re, im = result[m]
                    cosine, sine = twist[0, m, :, lanes2], twist[1, m, :, lanes2]
                    turned[m, row, lanes2] = re * cosine + im * sine
                    turned[m, row, lanes3] = im * cosine - re * sine

    def filtered(plan):
        lax.fori_loop(0, R2 // LANES, lambda half, carry: (columns(plan, half), carry)[1], 0)

    if len(plans) == 1:
        filtered(plans[0])
    else:
        pl.when(step == 0)(lambda: filtered(plans[0]))
        pl.when(step != 0)(lambda: filtered(plans[1]))

    @pl.when(step == pl.num_programs(0) - 1)
    def _():
        weights = table[...]
        low = lax.broadcasted_iota(jnp.int32, (R2, LANES), 1) < LANES // 2
        many = 4
        for m in range(0, R1, many):
            rows = turned[m : m + many].reshape(many * spectra * inputs, 2 * R2).astype(jnp.bfloat16)
            result = lax.dot_general(
                weights, rows, (((1,), (1,)), ((), ())), preferred_element_type=jnp.float32
            )
            for tile in range(many * spectra // 2):
                lanes = slice(tile * LANES, (tile + 1) * LANES)
                re, im = result[:R2, lanes], result[R2:, lanes]
                pair = (
                    jnp.where(low, re, pltpu.roll(im, LANES // 2, 1)),
                    jnp.where(low, pltpu.roll(re, LANES // 2, 1), im),
                )
                for e in range(2):
                    more, s = divmod(2 * tile + e, spectra)
                    spectrum[s, pl.ds(m + more, R2, stride=R1), :] = pair[e]

        def place(owner, carry):
            for slot in range(CAP):
                start = pl.multiple_of(first_ref[owner * CAP + slot], 8)
                rows = [p[owner, slot].astype(jnp.float32) for p in prior]
                rows += [spectrum[s, pl.ds(start, AVG), :] for s in range(spectra)]
                rows = rows[0] if len(rows) == 1 else jnp.concatenate(rows, axis=0)
                out[owner, slot] = rows.astype(jnp.bfloat16)
            return carry

        lax.fori_loop(0, out.shape[0], place, 0, unroll=2)


def channel_call(plans, first, xs, window, twist, table, prior=()):
    owners = (first.shape[0] - 1) // CAP
    block = 16
    inputs = max(x.shape[1] for x in xs)
    spectra = len(plans[0])

    def spec(x):
        skip, most = (inputs - x.shape[1]) // block, x.shape[1] // block - 1
        if most == 0:
            skip = 0
        return pl.BlockSpec((x.shape[0], block, F), lambda i, *_: (0, jnp.clip(i - skip, 0, most), 0))

    whole = lambda shape: pl.BlockSpec(shape, lambda i, *_: (0,) * len(shape))
    shape = (owners, CAP, (spectra + len(prior)) * AVG, LANES)
    return pl.pallas_call(
        functools.partial(channel_kernel, plans, len(xs)),
        out_shape=jax.ShapeDtypeStruct(shape, jnp.bfloat16),
        grid_spec=pltpu.PrefetchScalarGridSpec(
            num_scalar_prefetch=1,
            grid=(inputs // block,),
            in_specs=[spec(x) for x in xs] + [whole(x.shape) for x in (window, twist, table, *prior)],
            out_specs=whole(shape),
            scratch_shapes=[
                pltpu.VMEM((R1, spectra * inputs, 2 * R2), jnp.float32),
                pltpu.VMEM((spectra, F, LANES), jnp.float32),
            ],
        ),
        compiler_params=pltpu.CompilerParams(vmem_limit_bytes=VMEM),
        cost_estimate=pl.CostEstimate(flops=10**9 * spectra, bytes_accessed=8 * 2**20, transcendentals=0),
        name="channels",
    )(first, *xs, window, twist, table, *prior)


def correlate_kernel(n_tim, mixed, scale, valid_ref, piece, *refs):
    partial = refs[0] if len(refs) == 4 else None
    out, rows_k, rows_i = refs[-3:]
    slot, block = pl.program_id(0), pl.program_id(1)
    depth, width = rows_k.shape[1], rows_k.shape[2]
    tile = out.shape[1]
    blocks = width // tile
    half = depth // 2

    def arrange(which, q):
        lane = lax.broadcasted_iota(jnp.int32, (2 * AVG, LANES), 1)
        low, ahead = lane < LANES // 2, lane % (LANES // 2) < mixed
        lanes = pl.ds(pl.multiple_of(q * LANES, LANES), LANES)

        def rows(e, t):
            value = piece[(2 * q + e) * n_tim + t, which].astype(jnp.float32)
            if mixed:
                other = piece[(2 * q + e) * n_tim + (t + 1) % n_tim, which].astype(jnp.float32)
                value = jnp.where(ahead, other, value)
            return value

        base = 0
        for u in range(n_tim // 2):
            group = [[rows(e, 2 * u + v) for v in range(2)] for e in range(2)]
            for s in range(piece.shape[2] // AVG):
                even, odd = [
                    jnp.concatenate([group[e][v][AVG * s : AVG * s + AVG] for v in range(2)], axis=0)
                    for e in range(2)
                ]
                re = jnp.where(low, even, pltpu.roll(odd, LANES // 2, 1))
                im = jnp.where(low, pltpu.roll(even, LANES // 2, 1), odd)
                rows_k[which, base : base + 2 * AVG, lanes] = re.astype(jnp.bfloat16)
                rows_k[which, half + base : half + base + 2 * AVG, lanes] = im.astype(jnp.bfloat16)
                base += 2 * AVG
        turned = rows_k[which, :, lanes].T
        rows_i[which, lanes, :depth] = turned
        rows_i[which, lanes, depth:] = -turned[:, :half]

    @pl.when(jnp.logical_and(slot == 0, block == 0))
    def _():
        lax.fori_loop(0, width // LANES, lambda q, carry: (arrange(0, q), carry)[1], 0)

    def strip(which, i):
        upper = lax.broadcasted_iota(jnp.int32, (tile, tile), 0) <= lax.broadcasted_iota(
            jnp.int32, (tile, tile), 1
        )
        keep = valid_ref[which] != 0
        rows = slice(i * tile, (i + 1) * tile)
        for j in range(blocks):
            lanes = slice(j * tile, (j + 1) * tile)
            other = rows_k[which, :, lanes]
            real = imag = None
            if i <= j:
                real = jnp.dot(rows_i[which, rows, :depth], other, preferred_element_type=jnp.float32)
            if i >= j:
                imag = jnp.dot(rows_i[which, rows, half:], other, preferred_element_type=jnp.float32)
            value = real if imag is None else imag if real is None else jnp.where(upper, real, imag)
            if partial is not None:
                value = value + partial[0, :, lanes]
            out[0, :, lanes] = jnp.where(keep, value * scale, 0.0)

    each = width // LANES // blocks
    for which in range(CAP):
        for i in range(blocks):

            @pl.when(jnp.logical_and(slot == which, block == i))
            def _():
                if which + 1 < CAP:
                    for q in range(each):
                        arrange(which + 1, i * each + q)
                strip(which, i)


def correlate_call(n_inp, n_tim, mixed, scale, valid, piece, partial=None):
    width = n_inp * LANES // 2
    depth = n_tim * piece.shape[2] * 2
    tile = 256
    block = pl.BlockSpec((1, tile, width), lambda s, i, *_: (s, i, 0))
    more = [] if partial is None else [partial]
    return pl.pallas_call(
        functools.partial(correlate_kernel, n_tim, mixed, scale),
        out_shape=jax.ShapeDtypeStruct((CAP, width, width), jnp.float32),
        grid_spec=pltpu.PrefetchScalarGridSpec(
            num_scalar_prefetch=1,
            grid=(CAP, width // tile),
            in_specs=[pl.BlockSpec(piece.shape, lambda s, i, *_: (0, 0, 0, 0))] + [block] * len(more),
            out_specs=block,
            scratch_shapes=[
                pltpu.VMEM((CAP, depth, width), jnp.bfloat16),
                pltpu.VMEM((CAP, width, depth + depth // 2), jnp.bfloat16),
            ],
        ),
        compiler_params=pltpu.CompilerParams(vmem_limit_bytes=VMEM),
        cost_estimate=pl.CostEstimate(flops=5 * 10**9, bytes_accessed=19 * 2**20, transcendentals=0),
        name="correlate",
    )(valid, piece, *more)


def body(voltages, scale_exps, owner_table):
    n_inp = lax.axis_size("inp")
    n_tim = lax.axis_size("tim")
    devices = n_inp * n_tim
    spec_dev = voltages.shape[2] // F
    scale = jnp.exp2(scale_exps.astype(jnp.float32)) / 128.0
    own = [
        (voltages[:, :, s * F : (s + 1) * F].astype(jnp.float32) * scale[None, :, s : s + 1]).astype(
            jnp.bfloat16
        )
        for s in range(spec_dev)
    ]
    ahead = [(source, source + 1) for source in range(n_tim - 1)]
    back = [(source, (source - 1) % n_tim) for source in range(n_tim)]
    before = lax.ppermute(own[3], "tim", ahead)
    earlier = lax.ppermute(jnp.concatenate([own[1][:, :MIXED], own[2][:, :MIXED]]), "tim", ahead)
    after = lax.ppermute(jnp.concatenate([own[0][:, MIXED:], own[1][:, MIXED:]]), "tim", back)

    rows = owner_rows(owner_table, CAP)
    match = rows[None, :] == jnp.arange(devices * CAP, dtype=jnp.int32)[:, None]
    valid = jnp.any(match, axis=1).astype(jnp.int32)
    which = jnp.sum(jnp.where(match, jnp.arange(CH, dtype=jnp.int32)[None, :], 0), axis=1)
    first = (which * AVG - AVG * CH // 2) % F
    me = lax.axis_index("inp") * n_tim + lax.axis_index("tim")
    mine = lax.dynamic_slice(valid, (me * CAP,), (CAP,))

    window = jnp.asarray(window_table())
    twist = jnp.asarray(twist_table())
    table = jnp.asarray(radix_table()).astype(jnp.bfloat16)

    last = (lax.axis_index("tim") == n_tim - 1).astype(jnp.int32)
    first = jnp.concatenate([first, last[None]])
    tables = (window, twist, table)
    third = channel_call([[(((0, 0), (1, 0), (2, 0), (3, 0)), 0)]], first, own, *tables)
    second = [[(((3, 0), (0, 0), (1, 0), (2, 0)), 0)]]
    near = channel_call(second, first, (*own[:3], before), *tables, prior=(third,))
    near, earlier, after = lax.optimization_barrier((near, earlier, after))
    near = lax.all_to_all(near, ("inp", "tim"), split_axis=0, concat_axis=0, tiled=True)
    xs = (*own, before, earlier, after)
    e3, e2, e1, x0, x1, x2, x3, a0, a1 = (5, 0), (5, 2), (4, 0), (0, 0), (1, 0), (2, 0), (3, 0), (6, 0), (6, 2)
    plans = [
        [((e3, e2, e1, x0), 0), ((e2, e1, x0, x1), 0)],
        [((x1, x2, x3, a0), 3), ((x2, x3, a0, a1), 2)],
    ]
    far = channel_call(plans, first, xs, *tables)
    far = lax.all_to_all(far, ("inp", "tim"), split_axis=0, concat_axis=0, tiled=True)
    partial = correlate_call(n_inp, n_tim, 0, 1.0, mine, near)
    return correlate_call(n_inp, n_tim, MIXED, 1.0 / (n_tim * spec_dev * AVG), mine, far, partial)


def solution(mesh):
    return jax.shard_map(
        body,
        mesh=mesh,
        in_specs=(P(None, "inp", "tim"), P("inp", "tim"), P()),
        out_specs=P(("inp", "tim"), None, None),
        check_vma=False,
    )
```

```python
import functools
import math

import jax
import jax.numpy as jnp
import numpy as np
from jax import lax
from jax.experimental import pallas as pl
from jax.experimental.pallas import tpu as pltpu
from jax.sharding import PartitionSpec as P

F = 4096
AVG = 24
CH = 144
TAPS = 4
CAP = 2
R1 = 16
R2 = 256
LANES = 128
CHANNEL_VMEM = 30 * 2**20
CORRELATE_VMEM = 34 * 2**20
TILE = 256


def window_table():
    length = TAPS * F
    steps = np.arange(length, dtype=np.float64)
    centre = (steps + 0.5 - length / 2.0) / F
    taper = 0.5 - 0.5 * np.cos(2.0 * math.pi * (steps + 0.5) / length)
    table = (np.sinc(centre) * taper).reshape(TAPS, 1, F)
    table = np.concatenate([table, np.zeros((1, 1, F))], axis=0)
    return np.broadcast_to(table, (TAPS + 1, 8, F)).astype(np.float32)


def twist_table():
    phase = np.arange(R1)[:, None] * np.arange(R2)[None, :]
    angle = 2.0 * math.pi * phase / F
    table = np.stack([np.cos(angle), np.sin(angle)]) / math.sqrt(F)
    return np.broadcast_to(table[:, :, None, :], (2, R1, 8, R2)).astype(np.float32)


def radix_table():
    phase = np.arange(R2)[:, None] * np.arange(R2)[None, :] % R2
    angle = 2.0 * math.pi * phase / R2
    cosine, sine = np.cos(angle), np.sin(angle)
    table = np.concatenate(
        [np.concatenate([cosine, sine], axis=1), np.concatenate([-sine, cosine], axis=1)], axis=0
    )
    return table.astype(np.float32)


def owner_rows(owner_table, cap):
    index = jnp.arange(owner_table.shape[0], dtype=jnp.int32)
    same = owner_table[:, None] == owner_table[None, :]
    earlier = index[None, :] < index[:, None]
    slot = jnp.sum((same & earlier).astype(jnp.int32), axis=1)
    return owner_table * cap + slot


def four(a, b, c, d):
    sr, si = a[0] + c[0], a[1] + c[1]
    tr, ti = a[0] - c[0], a[1] - c[1]
    ur, ui = b[0] + d[0], b[1] + d[1]
    vr, vi = b[0] - d[0], b[1] - d[1]
    return (sr + ur, si + ui), (tr + vi, ti - vr), (sr - ur, si - ui), (tr - vi, ti + vr)


def turn(value, power):
    re, im = value
    power %= 16
    if power == 0:
        return value
    if power == 4:
        return im, -re
    root = math.sqrt(0.5)
    if power == 2:
        return (re + im) * root, (im - re) * root
    if power == 6:
        return (im - re) * root, (re + im) * (-root)
    cosine, sine = math.cos(2 * math.pi * power / 16), math.sin(2 * math.pi * power / 16)
    return re * cosine + im * sine, im * cosine - re * sine


def sixteen(x):
    inner = [four(x[b], x[4 + b], x[8 + b], x[12 + b]) for b in range(4)]
    out = [None] * 16
    for c in range(4):
        row = four(*[turn(inner[b][c], b * c) for b in range(4)])
        for d in range(4):
            out[c + 4 * d] = row[d]
    return out


def channel_kernel(plan, count, first_ref, *refs):
    xs, (window, twist, table) = refs[:count], refs[count : count + 3]
    prior, (out, turned, spectrum) = refs[count + 3 : -3], refs[-3:]
    step = pl.program_id(0)
    spectra = len(plan)
    block = 16
    inputs = turned.shape[1] // spectra
    slots = out.shape[0] * out.shape[1]
    wrapped = first_ref[slots] != 0

    def columns(half, carry):
        base = half * LANES
        members = pl.ds(pl.multiple_of(step * block, block), block)
        lanes2 = pl.ds(pl.multiple_of(base, LANES), LANES)
        lanes3 = pl.ds(pl.multiple_of(base + R2, LANES), LANES)
        for s, (blocks, cut) in enumerate(plan):
            for r in range(block // 8):
                series = []
                for n in range(R1):
                    lanes = pl.ds(pl.multiple_of(base + n * R2, LANES), LANES)
                    parts = []
                    for c in range(2):
                        total = None
                        for tap in range(TAPS):
                            index, place = blocks[tap]
                            shifted = pl.ds(pl.multiple_of(base + n * R2 + place * F, LANES), LANES)
                            value = xs[index][c, members, shifted].astype(jnp.float32)[8 * r : 8 * r + 8]
                            which = tap if tap >= cut else jnp.where(wrapped, TAPS, tap)
                            term = window[which, :, lanes] * value
                            total = term if total is None else total + term
                        parts.append(total.astype(jnp.bfloat16).astype(jnp.float32))
                    series.append(tuple(parts))
                result = sixteen(series)
                row = pl.ds(pl.multiple_of(step * block + s * inputs + 8 * r, 8), 8)
                for m in range(R1):
                    re, im = result[m]
                    cosine, sine = twist[0, m, :, lanes2], twist[1, m, :, lanes2]
                    turned[m, row, lanes2] = re * cosine + im * sine
                    turned[m, row, lanes3] = im * cosine - re * sine
        return carry

    lax.fori_loop(0, R2 // LANES, columns, 0)

    @pl.when(step == pl.num_programs(0) - 1)
    def _():
        weights = table[...]
        low = lax.broadcasted_iota(jnp.int32, (R2, LANES), 1) < LANES // 2
        many = 4
        for m in range(0, R1, many):
            rows = turned[m : m + many].reshape(many * spectra * inputs, 2 * R2).astype(jnp.bfloat16)
            result = lax.dot_general(
                weights, rows, (((1,), (1,)), ((), ())), preferred_element_type=jnp.float32
            )
            for tile in range(many * spectra // 2):
                lanes = slice(tile * LANES, (tile + 1) * LANES)
                re, im = result[:R2, lanes], result[R2:, lanes]
                pair = (
                    jnp.where(low, re, pltpu.roll(im, LANES // 2, 1)),
                    jnp.where(low, pltpu.roll(re, LANES // 2, 1), im),
                )
                for e in range(2):
                    more, s = divmod(2 * tile + e, spectra)
                    spectrum[s, pl.ds(m + more, R2, stride=R1), :] = pair[e]

        def place(owner, carry):
            for slot in range(CAP):
                start = pl.multiple_of(first_ref[owner * CAP + slot], 8)
                rows = [p[owner, slot].astype(jnp.float32) for p in prior]
                rows += [spectrum[s, pl.ds(start, AVG), :] for s in range(spectra)]
                rows = rows[0] if len(rows) == 1 else jnp.concatenate(rows, axis=0)
                out[owner, slot] = rows.astype(jnp.bfloat16)
            return carry

        lax.fori_loop(0, out.shape[0], place, 0, unroll=2)


def channel_call(plan, first, xs, window, twist, table, prior=()):
    owners = (first.shape[0] - 1) // CAP
    block = 16
    inputs = xs[0].shape[1]
    spectra = len(plan)
    held = pl.BlockSpec(memory_space=pltpu.VMEM)
    shape = (owners, CAP, (spectra + len(prior)) * AVG, LANES)
    return pl.pallas_call(
        functools.partial(channel_kernel, plan, len(xs)),
        out_shape=jax.ShapeDtypeStruct(shape, jnp.bfloat16),
        grid_spec=pltpu.PrefetchScalarGridSpec(
            num_scalar_prefetch=1,
            grid=(inputs // block,),
            in_specs=[held] * (len(xs) + 3 + len(prior)),
            out_specs=held,
            scratch_shapes=[
                pltpu.VMEM((R1, spectra * inputs, 2 * R2), jnp.float32),
                pltpu.VMEM((spectra, F, LANES), jnp.float32),
            ],
        ),
        compiler_params=pltpu.CompilerParams(vmem_limit_bytes=CHANNEL_VMEM),
        cost_estimate=pl.CostEstimate(flops=10**9 * spectra, bytes_accessed=8 * 2**20, transcendentals=0),
        name="channels",
    )(first, *xs, window, twist, table, *prior)


def correlate_kernel(n_tim, scale, valid_ref, piece, *refs):
    partial = refs[0] if len(refs) == 4 else None
    out, rows_k, rows_i = refs[-3:]
    slot, block = pl.program_id(0), pl.program_id(1)
    depth, width = rows_k.shape[1], rows_k.shape[2]
    held = partial is None
    tile = TILE
    blocks = width // tile
    half = depth // 2

    def arrange(which, q):
        lane = lax.broadcasted_iota(jnp.int32, (2 * AVG, LANES), 1)
        low = lane < LANES // 2
        lanes = pl.ds(pl.multiple_of(q * LANES, LANES), LANES)

        base = 0
        for u in range(n_tim // 2):
            group = [
                [piece[(2 * q + e) * n_tim + 2 * u + v, which].astype(jnp.float32) for v in range(2)]
                for e in range(2)
            ]
            for s in range(piece.shape[2] // AVG):
                even, odd = [
                    jnp.concatenate([group[e][v][AVG * s : AVG * s + AVG] for v in range(2)], axis=0)
                    for e in range(2)
                ]
                re = jnp.where(low, even, pltpu.roll(odd, LANES // 2, 1))
                im = jnp.where(low, pltpu.roll(even, LANES // 2, 1), odd)
                rows_k[which, base : base + 2 * AVG, lanes] = re.astype(jnp.bfloat16)
                rows_k[which, half + base : half + base + 2 * AVG, lanes] = im.astype(jnp.bfloat16)
                base += 2 * AVG
        turned = rows_k[which, :, lanes].T
        rows_i[which, lanes, :depth] = turned
        rows_i[which, lanes, depth:] = -turned[:, :half]

    @pl.when(jnp.logical_and(slot == 0, block == 0))
    def _():
        lax.fori_loop(0, width // LANES, lambda q, carry: (arrange(0, q), carry)[1], 0)

    def strip(which, i):
        upper = lax.broadcasted_iota(jnp.int32, (tile, tile), 0) <= lax.broadcasted_iota(
            jnp.int32, (tile, tile), 1
        )
        keep = valid_ref[which] != 0
        rows = slice(i * tile, (i + 1) * tile)
        for j in range(blocks):
            lanes = slice(j * tile, (j + 1) * tile)
            other = rows_k[which, :, lanes]
            real = imag = None
            if i <= j:
                real = jnp.dot(rows_i[which, rows, :depth], other, preferred_element_type=jnp.float32)
            if i >= j:
                imag = jnp.dot(rows_i[which, rows, half:], other, preferred_element_type=jnp.float32)
            value = real if imag is None else imag if real is None else jnp.where(upper, real, imag)
            if partial is not None:
                value = value + partial[which, rows, lanes]
            value = jnp.where(keep, value * scale, 0.0)
            if held:
                out[which, rows, lanes] = value
            else:
                out[0, :, lanes] = value

    each = width // LANES // blocks
    for which in range(CAP):
        for i in range(blocks):

            @pl.when(jnp.logical_and(slot == which, block == i))
            def _():
                if which + 1 < CAP:
                    for q in range(each):
                        arrange(which + 1, i * each + q)
                strip(which, i)


def correlate_call(n_inp, n_tim, scale, valid, piece, partial=None):
    width = n_inp * LANES // 2
    depth = n_tim * piece.shape[2] * 2
    tile = TILE
    block = pl.BlockSpec((1, tile, width), lambda s, i, *_: (s, i, 0))
    held = pl.BlockSpec(memory_space=pltpu.VMEM)
    more = [] if partial is None else [partial]
    return pl.pallas_call(
        functools.partial(correlate_kernel, n_tim, scale),
        out_shape=jax.ShapeDtypeStruct((CAP, width, width), jnp.float32),
        grid_spec=pltpu.PrefetchScalarGridSpec(
            num_scalar_prefetch=1,
            grid=(CAP, width // tile),
            in_specs=[held] + [held] * len(more),
            out_specs=block if more else held,
            scratch_shapes=[
                pltpu.VMEM((CAP, depth, width), jnp.bfloat16),
                pltpu.VMEM((CAP, width, depth + depth // 2), jnp.bfloat16),
            ],
        ),
        compiler_params=pltpu.CompilerParams(vmem_limit_bytes=CORRELATE_VMEM),
        cost_estimate=pl.CostEstimate(flops=5 * 10**9, bytes_accessed=19 * 2**20, transcendentals=0),
        name="correlate",
    )(valid, piece, *more)


def body(voltages, scale_exps, owner_table):
    n_inp = lax.axis_size("inp")
    n_tim = lax.axis_size("tim")
    devices = n_inp * n_tim
    spec_dev = voltages.shape[2] // F
    scale = jnp.exp2(scale_exps.astype(jnp.float32)) / 128.0
    lane = lax.broadcasted_iota(jnp.int32, (1, 1, 2 * F), 2)

    def samples(s, count):
        factor = scale[None, :, s : s + 1]
        if count == 2:
            factor = jnp.where(lane < F, factor, scale[None, :, s + 1 : s + 2])
        return (voltages[:, :, s * F : (s + count) * F].astype(jnp.float32) * factor).astype(jnp.bfloat16)

    own01, own2, own3 = samples(0, 2), samples(2, 1), samples(3, 1)
    ahead = [(source, source + 1) for source in range(n_tim - 1)]
    back = [(source, (source - 1) % n_tim) for source in range(n_tim)]
    before = lax.ppermute(own3, "tim", ahead)
    after = lax.ppermute(own01, "tim", back)

    rows = owner_rows(owner_table, CAP)
    match = rows[None, :] == jnp.arange(devices * CAP, dtype=jnp.int32)[:, None]
    valid = jnp.any(match, axis=1).astype(jnp.int32)
    which = jnp.sum(jnp.where(match, jnp.arange(CH, dtype=jnp.int32)[None, :], 0), axis=1)
    first = (which * AVG - AVG * CH // 2) % F
    me = lax.axis_index("inp") * n_tim + lax.axis_index("tim")
    mine = lax.dynamic_slice(valid, (me * CAP,), (CAP,))

    window = jnp.asarray(window_table())
    twist = jnp.asarray(twist_table())
    table = jnp.asarray(radix_table()).astype(jnp.bfloat16)

    last = (lax.axis_index("tim") == n_tim - 1).astype(jnp.int32)
    first = jnp.concatenate([first, last[None]])
    tables = (window, twist, table)
    x0, x1, x2, x3 = (0, 0), (0, 1), (1, 0), (2, 0)
    third = channel_call([((x0, x1, x2, x3), 0)], first, (own01, own2, own3), *tables)
    near = channel_call([(((2, 0), x0, x1, x2), 0)], first, (own01, own2, before), *tables, prior=(third,))
    near, after = lax.optimization_barrier((near, after))
    near = lax.all_to_all(near, ("inp", "tim"), split_axis=0, concat_axis=0, tiled=True)
    plan = [((x1, x2, x3, (3, 0)), 3), ((x2, x3, (3, 0), (3, 1)), 2)]
    far = channel_call(plan, first, (own01, own2, own3, after), *tables)
    far = lax.all_to_all(far, ("inp", "tim"), split_axis=0, concat_axis=0, tiled=True)
    partial = correlate_call(n_inp, n_tim, 1.0, mine, near)
    return correlate_call(n_inp, n_tim, 1.0 / (n_tim * spec_dev * AVG), mine, far, partial)


def solution(mesh):
    return jax.shard_map(
        body,
        mesh=mesh,
        in_specs=(P(None, "inp", "tim"), P("inp", "tim"), P()),
        out_specs=P(("inp", "tim"), None, None),
        check_vma=False,
    )
```

```python
import functools
import math

import jax
import jax.numpy as jnp
import numpy as np
from jax import lax
from jax.experimental import pallas as pl
from jax.experimental.pallas import tpu as pltpu
from jax.sharding import PartitionSpec as P

F = 4096
AVG = 24
CH = 144
TAPS = 4
CAP = 2
R1 = 16
R2 = 256
LANES = 128
CHANNEL_VMEM = 30 * 2**20
CORRELATE_VMEM = 34 * 2**20
TILE = 256


def row_table():
    length = TAPS * F
    steps = np.arange(length, dtype=np.float64)
    centre = (steps + 0.5 - length / 2.0) / F
    taper = 0.5 - 0.5 * np.cos(2.0 * math.pi * (steps + 0.5) / length)
    taps = (np.sinc(centre) * taper).reshape(TAPS, F)
    angle = 2.0 * math.pi * (np.arange(R1)[:, None] * np.arange(R2)[None, :]).reshape(1, F) / F
    rows = [taps, np.cos(angle) / math.sqrt(F), np.sin(angle) / math.sqrt(F), np.zeros((2, F))]
    return np.concatenate(rows, axis=0).astype(np.float32)


def radix_table():
    phase = np.arange(R2)[:, None] * np.arange(R2)[None, :] % R2
    angle = 2.0 * math.pi * phase / R2
    cosine, sine = np.cos(angle), np.sin(angle)
    table = np.concatenate(
        [np.concatenate([cosine, sine], axis=1), np.concatenate([-sine, cosine], axis=1)], axis=0
    )
    return table.astype(np.float32)


def owner_rows(owner_table, cap):
    index = jnp.arange(owner_table.shape[0], dtype=jnp.int32)
    same = owner_table[:, None] == owner_table[None, :]
    earlier = index[None, :] < index[:, None]
    slot = jnp.sum((same & earlier).astype(jnp.int32), axis=1)
    return owner_table * cap + slot


def four(a, b, c, d):
    sr, si = a[0] + c[0], a[1] + c[1]
    tr, ti = a[0] - c[0], a[1] - c[1]
    ur, ui = b[0] + d[0], b[1] + d[1]
    vr, vi = b[0] - d[0], b[1] - d[1]
    return (sr + ur, si + ui), (tr + vi, ti - vr), (sr - ur, si - ui), (tr - vi, ti + vr)


def turn(value, power):
    re, im = value
    power %= 16
    if power == 0:
        return value
    if power == 4:
        return im, -re
    root = math.sqrt(0.5)
    if power == 2:
        return (re + im) * root, (im - re) * root
    if power == 6:
        return (im - re) * root, (re + im) * (-root)
    cosine, sine = math.cos(2 * math.pi * power / 16), math.sin(2 * math.pi * power / 16)
    return re * cosine + im * sine, im * cosine - re * sine


def sixteen(x):
    inner = [four(x[b], x[4 + b], x[8 + b], x[12 + b]) for b in range(4)]
    out = [None] * 16
    for c in range(4):
        row = four(*[turn(inner[b][c], b * c) for b in range(4)])
        for d in range(4):
            out[c + 4 * d] = row[d]
    return out


def channel_kernel(plan, count, first_ref, *refs):
    xs, (rows_table, table) = refs[:count], refs[count : count + 2]
    prior, (out, turned, spectrum) = refs[count + 2 : -3], refs[-3:]
    step = pl.program_id(0)
    spectra = len(plan)
    block = 16
    inputs = turned.shape[1] // spectra
    slots = out.shape[0] * out.shape[1]
    wrapped = first_ref[slots] != 0

    def columns(half, carry):
        base = half * LANES
        members = pl.ds(pl.multiple_of(step * block, block), block)
        lanes2 = pl.ds(pl.multiple_of(base, LANES), LANES)
        lanes3 = pl.ds(pl.multiple_of(base + R2, LANES), LANES)
        for s, (blocks, cut) in enumerate(plan):
            for r in range(block // 8):
                series = []
                for n in range(R1):
                    lanes = pl.ds(pl.multiple_of(base + n * R2, LANES), LANES)
                    parts = []
                    for c in range(2):
                        total = None
                        for tap in range(TAPS):
                            index, place = blocks[tap]
                            shifted = pl.ds(pl.multiple_of(base + n * R2 + place * F, LANES), LANES)
                            value = xs[index][c, members, shifted].astype(jnp.float32)[8 * r : 8 * r + 8]
                            weight = rows_table[tap : tap + 1, lanes]
                            if tap < cut:
                                weight = jnp.where(wrapped, 0.0, weight)
                            term = weight * value
                            total = term if total is None else total + term
                        parts.append(total.astype(jnp.bfloat16).astype(jnp.float32))
                    series.append(tuple(parts))
                result = sixteen(series)
                row = pl.ds(pl.multiple_of(step * block + s * inputs + 8 * r, 8), 8)
                for m in range(R1):
                    re, im = result[m]
                    lanes = pl.ds(pl.multiple_of(base + m * R2, LANES), LANES)
                    cosine, sine = [rows_table[TAPS + k : TAPS + 1 + k, lanes] for k in range(2)]
                    turned[m, row, lanes2] = re * cosine + im * sine
                    turned[m, row, lanes3] = im * cosine - re * sine
        return carry

    lax.fori_loop(0, R2 // LANES, columns, 0)

    @pl.when(step == pl.num_programs(0) - 1)
    def _():
        weights = table[...]
        low = lax.broadcasted_iota(jnp.int32, (R2, LANES), 1) < LANES // 2
        many = 4
        for m in range(0, R1, many):
            rows = turned[m : m + many].reshape(many * spectra * inputs, 2 * R2).astype(jnp.bfloat16)
            result = lax.dot_general(
                weights, rows, (((1,), (1,)), ((), ())), preferred_element_type=jnp.float32
            )
            for tile in range(many * spectra // 2):
                lanes = slice(tile * LANES, (tile + 1) * LANES)
                re, im = result[:R2, lanes], result[R2:, lanes]
                pair = (
                    jnp.where(low, re, pltpu.roll(im, LANES // 2, 1)),
                    jnp.where(low, pltpu.roll(re, LANES // 2, 1), im),
                )
                for e in range(2):
                    more, s = divmod(2 * tile + e, spectra)
                    spectrum[s, pl.ds(m + more, R2, stride=R1), :] = pair[e]

        def place(owner, carry):
            for slot in range(CAP):
                start = pl.multiple_of(first_ref[owner * CAP + slot], 8)
                rows = [p[owner, slot].astype(jnp.float32) for p in prior]
                rows += [spectrum[s, pl.ds(start, AVG), :] for s in range(spectra)]
                rows = rows[0] if len(rows) == 1 else jnp.concatenate(rows, axis=0)
                out[owner, slot] = rows.astype(jnp.bfloat16)
            return carry

        lax.fori_loop(0, out.shape[0], place, 0, unroll=2)


def channel_call(plan, first, xs, rows_table, table, prior=()):
    owners = (first.shape[0] - 1) // CAP
    block = 16
    inputs = xs[0].shape[1]
    spectra = len(plan)
    held = pl.BlockSpec(memory_space=pltpu.VMEM)
    shape = (owners, CAP, (spectra + len(prior)) * AVG, LANES)
    return pl.pallas_call(
        functools.partial(channel_kernel, plan, len(xs)),
        out_shape=jax.ShapeDtypeStruct(shape, jnp.bfloat16),
        grid_spec=pltpu.PrefetchScalarGridSpec(
            num_scalar_prefetch=1,
            grid=(inputs // block,),
            in_specs=[held] * (len(xs) + 2 + len(prior)),
            out_specs=held,
            scratch_shapes=[
                pltpu.VMEM((R1, spectra * inputs, 2 * R2), jnp.float32),
                pltpu.VMEM((spectra, F, LANES), jnp.float32),
            ],
        ),
        compiler_params=pltpu.CompilerParams(vmem_limit_bytes=CHANNEL_VMEM),
        cost_estimate=pl.CostEstimate(flops=10**9 * spectra, bytes_accessed=8 * 2**20, transcendentals=0),
        name="channels",
    )(first, *xs, rows_table, table, *prior)


def correlate_kernel(n_tim, scale, valid_ref, piece, *refs):
    partial = refs[0] if len(refs) == 4 else None
    out, rows_k, rows_i = refs[-3:]
    slot, block = pl.program_id(0), pl.program_id(1)
    depth, width = rows_k.shape[1], rows_k.shape[2]
    held = partial is None
    tile = TILE
    blocks = width // tile
    half = depth // 2

    def arrange(which, q):
        lane = lax.broadcasted_iota(jnp.int32, (2 * AVG, LANES), 1)
        low = lane < LANES // 2
        lanes = pl.ds(pl.multiple_of(q * LANES, LANES), LANES)

        base = 0
        for u in range(n_tim // 2):
            group = [
                [piece[(2 * q + e) * n_tim + 2 * u + v, which].astype(jnp.float32) for v in range(2)]
                for e in range(2)
            ]
            for s in range(piece.shape[2] // AVG):
                even, odd = [
                    jnp.concatenate([group[e][v][AVG * s : AVG * s + AVG] for v in range(2)], axis=0)
                    for e in range(2)
                ]
                re = jnp.where(low, even, pltpu.roll(odd, LANES // 2, 1))
                im = jnp.where(low, pltpu.roll(even, LANES // 2, 1), odd)
                rows_k[which, base : base + 2 * AVG, lanes] = re.astype(jnp.bfloat16)
                rows_k[which, half + base : half + base + 2 * AVG, lanes] = im.astype(jnp.bfloat16)
                base += 2 * AVG
        turned = rows_k[which, :, lanes].T
        rows_i[which, lanes, :depth] = turned
        rows_i[which, lanes, depth:] = -turned[:, :half]

    @pl.when(jnp.logical_and(slot == 0, block == 0))
    def _():
        lax.fori_loop(0, width // LANES, lambda q, carry: (arrange(0, q), carry)[1], 0)

    def strip(which, i):
        upper = lax.broadcasted_iota(jnp.int32, (tile, tile), 0) <= lax.broadcasted_iota(
            jnp.int32, (tile, tile), 1
        )
        keep = valid_ref[which] != 0
        rows = slice(i * tile, (i + 1) * tile)
        for j in range(blocks):
            lanes = slice(j * tile, (j + 1) * tile)
            other = rows_k[which, :, lanes]
            real = imag = None
            if i <= j:
                real = jnp.dot(rows_i[which, rows, :depth], other, preferred_element_type=jnp.float32)
            if i >= j:
                imag = jnp.dot(rows_i[which, rows, half:], other, preferred_element_type=jnp.float32)
            value = real if imag is None else imag if real is None else jnp.where(upper, real, imag)
            if partial is not None:
                value = value + partial[which, rows, lanes].astype(jnp.float32)
            value = jnp.where(keep, value * scale, 0.0)
            if held:
                out[which, rows, lanes] = value.astype(out.dtype)
            else:
                out[0, :, lanes] = value

    each = width // LANES // blocks
    for which in range(CAP):
        for i in range(blocks):

            @pl.when(jnp.logical_and(slot == which, block == i))
            def _():
                if which + 1 < CAP:
                    for q in range(each):
                        arrange(which + 1, i * each + q)
                strip(which, i)


def correlate_call(n_inp, n_tim, scale, valid, piece, partial=None):
    width = n_inp * LANES // 2
    depth = n_tim * piece.shape[2] * 2
    tile = TILE
    block = pl.BlockSpec((1, tile, width), lambda s, i, *_: (s, i, 0))
    held = pl.BlockSpec(memory_space=pltpu.VMEM)
    more = [] if partial is None else [partial]
    return pl.pallas_call(
        functools.partial(correlate_kernel, n_tim, scale),
        out_shape=jax.ShapeDtypeStruct((CAP, width, width), jnp.float32 if more else jnp.bfloat16),
        grid_spec=pltpu.PrefetchScalarGridSpec(
            num_scalar_prefetch=1,
            grid=(CAP, width // tile),
            in_specs=[held] + [held] * len(more),
            out_specs=block if more else held,
            scratch_shapes=[
                pltpu.VMEM((CAP, depth, width), jnp.bfloat16),
                pltpu.VMEM((CAP, width, depth + depth // 2), jnp.bfloat16),
            ],
        ),
        compiler_params=pltpu.CompilerParams(vmem_limit_bytes=CORRELATE_VMEM),
        cost_estimate=pl.CostEstimate(flops=5 * 10**9, bytes_accessed=19 * 2**20, transcendentals=0),
        name="correlate",
    )(valid, piece, *more)


def body(voltages, scale_exps, owner_table):
    n_inp = lax.axis_size("inp")
    n_tim = lax.axis_size("tim")
    devices = n_inp * n_tim
    spec_dev = voltages.shape[2] // F
    scale = jnp.exp2(scale_exps.astype(jnp.float32)) / 128.0
    lane = lax.broadcasted_iota(jnp.int32, (1, 1, 2 * F), 2)

    def samples(s, count):
        factor = scale[None, :, s : s + 1]
        if count == 2:
            factor = jnp.where(lane < F, factor, scale[None, :, s + 1 : s + 2])
        return (voltages[:, :, s * F : (s + count) * F].astype(jnp.float32) * factor).astype(jnp.bfloat16)

    own01, own2, own3 = samples(0, 2), samples(2, 1), samples(3, 1)
    ahead = [(source, source + 1) for source in range(n_tim - 1)]
    back = [(source, (source - 1) % n_tim) for source in range(n_tim)]
    own01, own3 = lax.optimization_barrier((own01, own3))
    before = lax.ppermute(own3, "tim", ahead)
    after = lax.ppermute(own01, "tim", back)

    rows = owner_rows(owner_table, CAP)
    match = rows[None, :] == jnp.arange(devices * CAP, dtype=jnp.int32)[:, None]
    valid = jnp.any(match, axis=1).astype(jnp.int32)
    which = jnp.sum(jnp.where(match, jnp.arange(CH, dtype=jnp.int32)[None, :], 0), axis=1)
    first = (which * AVG - AVG * CH // 2) % F
    me = lax.axis_index("inp") * n_tim + lax.axis_index("tim")
    mine = lax.dynamic_slice(valid, (me * CAP,), (CAP,))

    table = jnp.asarray(radix_table()).astype(jnp.bfloat16)

    last = (lax.axis_index("tim") == n_tim - 1).astype(jnp.int32)
    first = jnp.concatenate([first, last[None]])
    tables = (jnp.asarray(row_table()), table)
    x0, x1, x2, x3 = (0, 0), (0, 1), (1, 0), (2, 0)
    third = channel_call([((x0, x1, x2, x3), 0)], first, (own01, own2, own3), *tables)
    near = channel_call([(((2, 0), x0, x1, x2), 0)], first, (own01, own2, before), *tables, prior=(third,))
    near, after = lax.optimization_barrier((near, after))
    near = lax.all_to_all(near, ("inp", "tim"), split_axis=0, concat_axis=0, tiled=True)
    plan = [((x1, x2, x3, (3, 0)), 3), ((x2, x3, (3, 0), (3, 1)), 2)]
    far = channel_call(plan, first, (own01, own2, own3, after), *tables)
    far = lax.all_to_all(far, ("inp", "tim"), split_axis=0, concat_axis=0, tiled=True)
    partial = correlate_call(n_inp, n_tim, 1.0, mine, near)
    return correlate_call(n_inp, n_tim, 1.0 / (n_tim * spec_dev * AVG), mine, far, partial)


def solution(mesh):
    return jax.shard_map(
        body,
        mesh=mesh,
        in_specs=(P(None, "inp", "tim"), P("inp", "tim"), P()),
        out_specs=P(("inp", "tim"), None, None),
        check_vma=False,
    )
```

```python
import functools
import math

import jax
import jax.numpy as jnp
import numpy as np
from jax import lax
from jax.experimental import pallas as pl
from jax.experimental.pallas import tpu as pltpu
from jax.sharding import PartitionSpec as P

F = 4096
AVG = 24
CH = 144
TAPS = 4
CAP = 2
R1 = 16
R2 = 256
LANES = 128
CHANNEL_VMEM = 30 * 2**20
CORRELATE_VMEM = 50 * 2**20
TILE = 256


def row_table():
    length = TAPS * F
    steps = np.arange(length, dtype=np.float64)
    centre = (steps + 0.5 - length / 2.0) / F
    taper = 0.5 - 0.5 * np.cos(2.0 * math.pi * (steps + 0.5) / length)
    taps = (np.sinc(centre) * taper).reshape(TAPS, F)
    angle = 2.0 * math.pi * (np.arange(R1)[:, None] * np.arange(R2)[None, :]).reshape(1, F) / F
    rows = [taps, np.cos(angle) / math.sqrt(F), np.sin(angle) / math.sqrt(F), np.zeros((2, F))]
    return np.concatenate(rows, axis=0).astype(np.float32)


def radix_table():
    phase = np.arange(R2)[:, None] * np.arange(R2)[None, :] % R2
    angle = 2.0 * math.pi * phase / R2
    cosine, sine = np.cos(angle), np.sin(angle)
    table = np.concatenate(
        [np.concatenate([cosine, sine], axis=1), np.concatenate([-sine, cosine], axis=1)], axis=0
    )
    return table.astype(np.float32)


def owner_rows(owner_table, cap):
    index = jnp.arange(owner_table.shape[0], dtype=jnp.int32)
    same = owner_table[:, None] == owner_table[None, :]
    earlier = index[None, :] < index[:, None]
    slot = jnp.sum((same & earlier).astype(jnp.int32), axis=1)
    return owner_table * cap + slot


def four(a, b, c, d):
    sr, si = a[0] + c[0], a[1] + c[1]
    tr, ti = a[0] - c[0], a[1] - c[1]
    ur, ui = b[0] + d[0], b[1] + d[1]
    vr, vi = b[0] - d[0], b[1] - d[1]
    return (sr + ur, si + ui), (tr + vi, ti - vr), (sr - ur, si - ui), (tr - vi, ti + vr)


def turn(value, power):
    re, im = value
    power %= 16
    if power == 0:
        return value
    if power == 4:
        return im, -re
    root = math.sqrt(0.5)
    if power == 2:
        return (re + im) * root, (im - re) * root
    if power == 6:
        return (im - re) * root, (re + im) * (-root)
    cosine, sine = math.cos(2 * math.pi * power / 16), math.sin(2 * math.pi * power / 16)
    return re * cosine + im * sine, im * cosine - re * sine


def sixteen(x):
    inner = [four(x[b], x[4 + b], x[8 + b], x[12 + b]) for b in range(4)]
    out = [None] * 16
    for c in range(4):
        row = four(*[turn(inner[b][c], b * c) for b in range(4)])
        for d in range(4):
            out[c + 4 * d] = row[d]
    return out


def channel_kernel(plan, count, first_ref, *refs):
    xs, (rows_table, table) = refs[:count], refs[count : count + 2]
    prior, (out, turned, spectrum) = refs[count + 2 : -3], refs[-3:]
    step = pl.program_id(0)
    spectra = len(plan)
    block = 16
    inputs = turned.shape[1] // spectra
    slots = out.shape[0] * out.shape[1]
    wrapped = first_ref[slots] != 0

    def columns(s, blocks, cut, half):
        base = half * LANES
        lanes2 = pl.ds(pl.multiple_of(base, LANES), LANES)
        lanes3 = pl.ds(pl.multiple_of(base + R2, LANES), LANES)
        for r in range(block // 8):
            series = []
            for n in range(R1):
                lanes = pl.ds(pl.multiple_of(base + n * R2, LANES), LANES)
                parts = []
                for c in range(2):
                    total = None
                    for tap in range(TAPS):
                        index, skip = blocks[tap]
                        members = pl.ds(pl.multiple_of(step * block - skip, block), block)
                        value = xs[index][c, members, lanes].astype(jnp.float32)[8 * r : 8 * r + 8]
                        weight = rows_table[tap : tap + 1, lanes]
                        if tap < cut:
                            weight = jnp.where(wrapped, 0.0, weight)
                        term = weight * value
                        total = term if total is None else total + term
                    parts.append(total.astype(jnp.bfloat16).astype(jnp.float32))
                series.append(tuple(parts))
            result = sixteen(series)
            row = pl.ds(pl.multiple_of(step * block + s * inputs + 8 * r, 8), 8)
            for m in range(R1):
                re, im = result[m]
                lanes = pl.ds(pl.multiple_of(base + m * R2, LANES), LANES)
                cosine, sine = [rows_table[TAPS + k : TAPS + 1 + k, lanes] for k in range(2)]
                turned[m, row, lanes2] = re * cosine + im * sine
                turned[m, row, lanes3] = im * cosine - re * sine

    def filtered(s, blocks, cut):
        lax.fori_loop(0, R2 // LANES, lambda half, carry: (columns(s, blocks, cut, half), carry)[1], 0)

    middle = pl.num_programs(0) // 2
    for s, options in enumerate(plan):
        if len(options) == 1:
            filtered(s, *options[0])
        else:
            pl.when(step < middle)(functools.partial(filtered, s, *options[0]))
            pl.when(step >= middle)(functools.partial(filtered, s, *options[1]))

    @pl.when(step == pl.num_programs(0) - 1)
    def _():
        weights = table[...]
        low = lax.broadcasted_iota(jnp.int32, (R2, LANES), 1) < LANES // 2
        many = 4
        for m in range(0, R1, many):
            rows = turned[m : m + many].reshape(many * spectra * inputs, 2 * R2).astype(jnp.bfloat16)
            result = lax.dot_general(
                weights, rows, (((1,), (1,)), ((), ())), preferred_element_type=jnp.float32
            )
            for tile in range(many * spectra // 2):
                lanes = slice(tile * LANES, (tile + 1) * LANES)
                re, im = result[:R2, lanes], result[R2:, lanes]
                pair = (
                    jnp.where(low, re, pltpu.roll(im, LANES // 2, 1)),
                    jnp.where(low, pltpu.roll(re, LANES // 2, 1), im),
                )
                for e in range(2):
                    more, s = divmod(2 * tile + e, spectra)
                    spectrum[s, pl.ds(m + more, R2, stride=R1), :] = pair[e]

        def place(owner, carry):
            for slot in range(CAP):
                start = pl.multiple_of(first_ref[owner * CAP + slot], 8)
                rows = [p[owner, slot].astype(jnp.float32) for p in prior]
                rows += [spectrum[s, pl.ds(start, AVG), :] for s in range(spectra)]
                rows = rows[0] if len(rows) == 1 else jnp.concatenate(rows, axis=0)
                out[owner, slot] = rows.astype(jnp.bfloat16)
            return carry

        lax.fori_loop(0, out.shape[0], place, 0, unroll=2)


def channel_call(plan, first, xs, rows_table, table, prior=()):
    owners = (first.shape[0] - 1) // CAP
    block = 16
    inputs = xs[0].shape[1]
    spectra = len(plan)
    held = pl.BlockSpec(memory_space=pltpu.VMEM)
    shape = (owners, CAP, (spectra + len(prior)) * AVG, LANES)
    return pl.pallas_call(
        functools.partial(channel_kernel, plan, len(xs)),
        out_shape=jax.ShapeDtypeStruct(shape, jnp.bfloat16),
        grid_spec=pltpu.PrefetchScalarGridSpec(
            num_scalar_prefetch=1,
            grid=(inputs // block,),
            in_specs=[held] * (len(xs) + 2 + len(prior)),
            out_specs=held,
            scratch_shapes=[
                pltpu.VMEM((R1, spectra * inputs, 2 * R2), jnp.float32),
                pltpu.VMEM((spectra, F, LANES), jnp.float32),
            ],
        ),
        compiler_params=pltpu.CompilerParams(vmem_limit_bytes=CHANNEL_VMEM),
        cost_estimate=pl.CostEstimate(flops=10**9 * spectra, bytes_accessed=8 * 2**20, transcendentals=0),
        name="channels",
    )(first, *xs, rows_table, table, *prior)


def correlate_kernel(n_tim, mixed, scale, valid_ref, piece, *refs):
    if len(refs) == 6:
        partial_hbm, out, rows_k, rows_i, partial, arrived = refs
        fetch = [pltpu.make_async_copy(partial_hbm.at[k], partial.at[k], arrived.at[k]) for k in range(CAP)]
    else:
        out, rows_k, rows_i = refs
        partial = fetch = None
    slot, block = pl.program_id(0), pl.program_id(1)
    depth, width = rows_k.shape[1], rows_k.shape[2]
    held = partial is None
    tile = TILE
    blocks = width // tile
    half = depth // 2

    def arrange(which, q):
        lane = lax.broadcasted_iota(jnp.int32, (2 * AVG, LANES), 1)
        low, lower = lane < LANES // 2, lane % (LANES // 2) < LANES // 4
        lanes = pl.ds(pl.multiple_of(q * LANES, LANES), LANES)

        base = 0
        for u in range(n_tim // 2):
            group = [
                [piece[(2 * q + e) * n_tim + 2 * u + v, which].astype(jnp.float32) for v in range(2)]
                for e in range(2)
            ]
            if mixed:
                for e in range(2):
                    for v in range(2):
                        later = (2 * u + v + 1) % n_tim
                        other = piece[(2 * q + e) * n_tim + later, which].astype(jnp.float32)[AVG:]
                        mine = group[e][v]
                        turn = jnp.where(lower[:AVG], other, mine[AVG:])
                        group[e][v] = jnp.concatenate([mine[:AVG], turn], axis=0)
            for s in range(piece.shape[2] // AVG):
                even, odd = [
                    jnp.concatenate([group[e][v][AVG * s : AVG * s + AVG] for v in range(2)], axis=0)
                    for e in range(2)
                ]
                re = jnp.where(low, even, pltpu.roll(odd, LANES // 2, 1))
                im = jnp.where(low, pltpu.roll(even, LANES // 2, 1), odd)
                rows_k[which, base : base + 2 * AVG, lanes] = re.astype(jnp.bfloat16)
                rows_k[which, half + base : half + base + 2 * AVG, lanes] = im.astype(jnp.bfloat16)
                base += 2 * AVG
        turned = rows_k[which, :, lanes].T
        rows_i[which, lanes, :depth] = turned
        rows_i[which, lanes, depth:] = -turned[:, :half]

    @pl.when(jnp.logical_and(slot == 0, block == 0))
    def _():
        if fetch is not None:
            for copy in fetch:
                copy.start()
        lax.fori_loop(0, width // LANES, lambda q, carry: (arrange(0, q), carry)[1], 0)

    if fetch is not None:
        for which in range(CAP):
            pl.when(jnp.logical_and(slot == which, block == 0))(fetch[which].wait)

    def strip(which, i):
        upper = lax.broadcasted_iota(jnp.int32, (tile, tile), 0) <= lax.broadcasted_iota(
            jnp.int32, (tile, tile), 1
        )
        keep = valid_ref[which] != 0
        rows = slice(i * tile, (i + 1) * tile)
        for j in range(blocks):
            lanes = slice(j * tile, (j + 1) * tile)
            other = rows_k[which, :, lanes]
            real = imag = None
            if i <= j:
                real = jnp.dot(rows_i[which, rows, :depth], other, preferred_element_type=jnp.float32)
            if i >= j:
                imag = jnp.dot(rows_i[which, rows, half:], other, preferred_element_type=jnp.float32)
            value = real if imag is None else imag if real is None else jnp.where(upper, real, imag)
            if partial is not None:
                value = value + partial[which, rows, lanes].astype(jnp.float32)
            value = jnp.where(keep, value * scale, 0.0)
            if held:
                out[which, rows, lanes] = value.astype(out.dtype)
            else:
                out[0, :, lanes] = value

    each = width // LANES // blocks
    for which in range(CAP):
        for i in range(blocks):

            @pl.when(jnp.logical_and(slot == which, block == i))
            def _():
                if which + 1 < CAP:
                    for q in range(each):
                        arrange(which + 1, i * each + q)
                strip(which, i)


def correlate_call(n_inp, n_tim, mixed, scale, valid, piece, partial=None):
    width = n_inp * LANES // 2
    depth = n_tim * piece.shape[2] * 2
    tile = TILE
    block = pl.BlockSpec((1, tile, width), lambda s, i, *_: (s, i, 0))
    held = pl.BlockSpec(memory_space=pltpu.VMEM)
    more = [] if partial is None else [partial]
    return pl.pallas_call(
        functools.partial(correlate_kernel, n_tim, mixed, scale),
        out_shape=jax.ShapeDtypeStruct((CAP, width, width), jnp.float32 if more else jnp.bfloat16),
        grid_spec=pltpu.PrefetchScalarGridSpec(
            num_scalar_prefetch=1,
            grid=(CAP, width // tile),
            in_specs=[held] + [pl.BlockSpec(memory_space=pl.ANY)] * len(more),
            out_specs=block if more else held,
            scratch_shapes=[
                pltpu.VMEM((CAP, depth, width), jnp.bfloat16),
                pltpu.VMEM((CAP, width, depth + depth // 2), jnp.bfloat16),
            ]
            + [pltpu.VMEM(p.shape, p.dtype) for p in more]
            + [pltpu.SemaphoreType.DMA((CAP,)) for _ in more],
        ),
        compiler_params=pltpu.CompilerParams(vmem_limit_bytes=CORRELATE_VMEM),
        cost_estimate=pl.CostEstimate(flops=5 * 10**9, bytes_accessed=19 * 2**20, transcendentals=0),
        name="correlate",
    )(valid, piece, *more)


def body(voltages, scale_exps, owner_table):
    n_inp = lax.axis_size("inp")
    n_tim = lax.axis_size("tim")
    devices = n_inp * n_tim
    spec_dev = voltages.shape[2] // F
    scale = jnp.exp2(scale_exps.astype(jnp.float32)) / 128.0
    own = [
        (voltages[:, :, s * F : (s + 1) * F].astype(jnp.float32) * scale[None, :, s : s + 1]).astype(
            jnp.bfloat16
        )
        for s in range(spec_dev)
    ]
    ahead = [(source, source + 1) for source in range(n_tim - 1)]
    back = [(source, (source - 1) % n_tim) for source in range(n_tim)]
    half = voltages.shape[1] // 2
    minus1 = lax.ppermute(own[3], "tim", ahead)
    plus0 = lax.ppermute(own[0], "tim", back)
    minus2 = lax.ppermute(own[2][:, :half], "tim", ahead)
    plus1 = lax.ppermute(own[1][:, half:], "tim", back)

    rows = owner_rows(owner_table, CAP)
    match = rows[None, :] == jnp.arange(devices * CAP, dtype=jnp.int32)[:, None]
    valid = jnp.any(match, axis=1).astype(jnp.int32)
    which = jnp.sum(jnp.where(match, jnp.arange(CH, dtype=jnp.int32)[None, :], 0), axis=1)
    first = (which * AVG - AVG * CH // 2) % F
    me = lax.axis_index("inp") * n_tim + lax.axis_index("tim")
    mine = lax.dynamic_slice(valid, (me * CAP,), (CAP,))

    table = jnp.asarray(radix_table()).astype(jnp.bfloat16)

    last = (lax.axis_index("tim") == n_tim - 1).astype(jnp.int32)
    first = jnp.concatenate([first, last[None]])
    tables = (jnp.asarray(row_table()), table)
    x0, x1, x2, x3 = [(s, 0) for s in range(spec_dev)]
    third = channel_call([[((x0, x1, x2, x3), 0)]], first, own, *tables)
    near = channel_call([[(((3, 0), x0, x1, x2), 0)]], first, (*own[:3], minus1), *tables, prior=(third,))
    near, plus0, minus2, plus1 = lax.optimization_barrier((near, plus0, minus2, plus1))
    near = lax.all_to_all(near, ("inp", "tim"), split_axis=0, concat_axis=0, tiled=True)
    m1, m2, p0, p1 = (4, 0), (5, 0), (6, 0), (7, half)
    plan = [[((x1, x2, x3, p0), 3)], [((m2, m1, x0, x1), 0), ((x2, x3, p0, p1), 2)]]
    far = channel_call(plan, first, (*own, minus1, minus2, plus0, plus1), *tables)
    far = lax.all_to_all(far, ("inp", "tim"), split_axis=0, concat_axis=0, tiled=True)
    partial = correlate_call(n_inp, n_tim, False, 1.0, mine, near)
    return correlate_call(n_inp, n_tim, True, 1.0 / (n_tim * spec_dev * AVG), mine, far, partial)


def solution(mesh):
    return jax.shard_map(
        body,
        mesh=mesh,
        in_specs=(P(None, "inp", "tim"), P("inp", "tim"), P()),
        out_specs=P(("inp", "tim"), None, None),
        check_vma=False,
    )
```

```python
import functools
import math

import jax
import jax.numpy as jnp
import numpy as np
from jax import lax
from jax.experimental import pallas as pl
from jax.experimental.pallas import tpu as pltpu
from jax.sharding import PartitionSpec as P

F = 4096
AVG = 24
CH = 144
TAPS = 4
CAP = 2
R1 = 16
R2 = 256
LANES = 128
SAMPLE_VMEM = 46 * 2**20
CHANNEL_VMEM = 30 * 2**20
CORRELATE_VMEM = 50 * 2**20
TILE = 256


def row_table():
    length = TAPS * F
    steps = np.arange(length, dtype=np.float64)
    centre = (steps + 0.5 - length / 2.0) / F
    taper = 0.5 - 0.5 * np.cos(2.0 * math.pi * (steps + 0.5) / length)
    taps = (np.sinc(centre) * taper).reshape(TAPS, F)
    angle = 2.0 * math.pi * (np.arange(R1)[:, None] * np.arange(R2)[None, :]).reshape(1, F) / F
    rows = [taps, np.cos(angle) / math.sqrt(F), np.sin(angle) / math.sqrt(F), np.zeros((2, F))]
    return np.concatenate(rows, axis=0).astype(np.float32)


def radix_table():
    phase = np.arange(R2)[:, None] * np.arange(R2)[None, :] % R2
    angle = 2.0 * math.pi * phase / R2
    cosine, sine = np.cos(angle), np.sin(angle)
    table = np.concatenate(
        [np.concatenate([cosine, sine], axis=1), np.concatenate([-sine, cosine], axis=1)], axis=0
    )
    return table.astype(np.float32)


def owner_rows(owner_table, cap):
    index = jnp.arange(owner_table.shape[0], dtype=jnp.int32)
    same = owner_table[:, None] == owner_table[None, :]
    earlier = index[None, :] < index[:, None]
    slot = jnp.sum((same & earlier).astype(jnp.int32), axis=1)
    return owner_table * cap + slot


def four(a, b, c, d):
    sr, si = a[0] + c[0], a[1] + c[1]
    tr, ti = a[0] - c[0], a[1] - c[1]
    ur, ui = b[0] + d[0], b[1] + d[1]
    vr, vi = b[0] - d[0], b[1] - d[1]
    return (sr + ur, si + ui), (tr + vi, ti - vr), (sr - ur, si - ui), (tr - vi, ti + vr)


def turn(value, power):
    re, im = value
    power %= 16
    if power == 0:
        return value
    if power == 4:
        return im, -re
    root = math.sqrt(0.5)
    if power == 2:
        return (re + im) * root, (im - re) * root
    if power == 6:
        return (im - re) * root, (re + im) * (-root)
    cosine, sine = math.cos(2 * math.pi * power / 16), math.sin(2 * math.pi * power / 16)
    return re * cosine + im * sine, im * cosine - re * sine


def sixteen(x):
    inner = [four(x[b], x[4 + b], x[8 + b], x[12 + b]) for b in range(4)]
    out = [None] * 16
    for c in range(4):
        row = four(*[turn(inner[b][c], b * c) for b in range(4)])
        for d in range(4):
            out[c + 4 * d] = row[d]
    return out


def sample_kernel(exps, voltages, *outs):
    wholes, low2, high1 = outs[:-2], outs[-2], outs[-1]
    step, block = pl.program_id(0), voltages.shape[1]
    half = low2.shape[1]
    rows = pl.ds(pl.multiple_of(step * block, block), block)
    factor = jnp.left_shift(1, exps[rows, :]).astype(jnp.float32) * (1.0 / 128.0)
    for s, whole in enumerate(wholes):
        for c in range(2):
            value = voltages[c, :, s * F : (s + 1) * F].astype(jnp.float32) * factor[:, s : s + 1]
            value = value.astype(jnp.bfloat16)
            whole[c, rows, :] = value
            if s == 2:

                @pl.when(step * block < half)
                def _():
                    low2[c, rows, :] = value

            if s == 1:

                @pl.when(step * block >= half)
                def _():
                    high1[c, pl.ds(pl.multiple_of(step * block - half, block), block), :] = value


def sample_call(voltages, exps):
    inputs, spectra = exps.shape
    block = 16
    held = pl.BlockSpec(memory_space=pltpu.VMEM)
    shapes = [(2, inputs, F)] * spectra + [(2, inputs // 2, F)] * 2
    return pl.pallas_call(
        sample_kernel,
        out_shape=[jax.ShapeDtypeStruct(shape, jnp.bfloat16) for shape in shapes],
        grid=(inputs // block,),
        in_specs=[held, pl.BlockSpec((2, block, spectra * F), lambda i: (0, i, 0))],
        out_specs=[held] * len(shapes),
        compiler_params=pltpu.CompilerParams(vmem_limit_bytes=SAMPLE_VMEM),
        cost_estimate=pl.CostEstimate(flops=10**7, bytes_accessed=13 * 2**20, transcendentals=0),
        name="samples",
    )(exps, voltages)


def channel_kernel(plan, count, first_ref, *refs):
    xs, (rows_table, table) = refs[:count], refs[count : count + 2]
    prior, (out, turned, spectrum) = refs[count + 2 : -3], refs[-3:]
    step = pl.program_id(0)
    spectra = len(plan)
    block = 16
    inputs = turned.shape[1] // spectra
    slots = out.shape[0] * out.shape[1]
    wrapped = first_ref[slots] != 0

    def columns(s, blocks, cut, half):
        base = half * LANES
        lanes2 = pl.ds(pl.multiple_of(base, LANES), LANES)
        lanes3 = pl.ds(pl.multiple_of(base + R2, LANES), LANES)
        for r in range(block // 8):
            series = []
            for n in range(R1):
                lanes = pl.ds(pl.multiple_of(base + n * R2, LANES), LANES)
                parts = []
                for c in range(2):
                    total = None
                    for tap in range(TAPS):
                        index, skip = blocks[tap]
                        members = pl.ds(pl.multiple_of(step * block - skip, block), block)
                        value = xs[index][c, members, lanes].astype(jnp.float32)[8 * r : 8 * r + 8]
                        weight = rows_table[tap : tap + 1, lanes]
                        if tap < cut:
                            weight = jnp.where(wrapped, 0.0, weight)
                        term = weight * value
                        total = term if total is None else total + term
                    parts.append(total.astype(jnp.bfloat16).astype(jnp.float32))
                series.append(tuple(parts))
            result = sixteen(series)
            row = pl.ds(pl.multiple_of(step * block + s * inputs + 8 * r, 8), 8)
            for m in range(R1):
                re, im = result[m]
                lanes = pl.ds(pl.multiple_of(base + m * R2, LANES), LANES)
                cosine, sine = [rows_table[TAPS + k : TAPS + 1 + k, lanes] for k in range(2)]
                turned[m, row, lanes2] = re * cosine + im * sine
                turned[m, row, lanes3] = im * cosine - re * sine

    def filtered(s, blocks, cut):
        lax.fori_loop(0, R2 // LANES, lambda half, carry: (columns(s, blocks, cut, half), carry)[1], 0)

    middle = pl.num_programs(0) // 2
    for s, options in enumerate(plan):
        if len(options) == 1:
            filtered(s, *options[0])
        else:
            pl.when(step < middle)(functools.partial(filtered, s, *options[0]))
            pl.when(step >= middle)(functools.partial(filtered, s, *options[1]))

    @pl.when(step == pl.num_programs(0) - 1)
    def _():
        weights = table[...]
        low = lax.broadcasted_iota(jnp.int32, (R2, LANES), 1) < LANES // 2
        many = 4
        for m in range(0, R1, many):
            rows = turned[m : m + many].reshape(many * spectra * inputs, 2 * R2).astype(jnp.bfloat16)
            result = lax.dot_general(
                weights, rows, (((1,), (1,)), ((), ())), preferred_element_type=jnp.float32
            )
            for tile in range(many * spectra // 2):
                lanes = slice(tile * LANES, (tile + 1) * LANES)
                re, im = result[:R2, lanes], result[R2:, lanes]
                pair = (
                    jnp.where(low, re, pltpu.roll(im, LANES // 2, 1)),
                    jnp.where(low, pltpu.roll(re, LANES // 2, 1), im),
                )
                for e in range(2):
                    more, s = divmod(2 * tile + e, spectra)
                    spectrum[s, pl.ds(m + more, R2, stride=R1), :] = pair[e]

        def place(owner, carry):
            for slot in range(CAP):
                start = pl.multiple_of(first_ref[owner * CAP + slot], 8)
                rows = [p[owner, slot].astype(jnp.float32) for p in prior]
                rows += [spectrum[s, pl.ds(start, AVG), :] for s in range(spectra)]
                rows = rows[0] if len(rows) == 1 else jnp.concatenate(rows, axis=0)
                out[owner, slot] = rows.astype(jnp.bfloat16)
            return carry

        lax.fori_loop(0, out.shape[0], place, 0, unroll=2)


def channel_call(plan, first, xs, rows_table, table, prior=()):
    owners = (first.shape[0] - 1) // CAP
    block = 16
    inputs = xs[0].shape[1]
    spectra = len(plan)
    held = pl.BlockSpec(memory_space=pltpu.VMEM)
    shape = (owners, CAP, (spectra + len(prior)) * AVG, LANES)
    return pl.pallas_call(
        functools.partial(channel_kernel, plan, len(xs)),
        out_shape=jax.ShapeDtypeStruct(shape, jnp.bfloat16),
        grid_spec=pltpu.PrefetchScalarGridSpec(
            num_scalar_prefetch=1,
            grid=(inputs // block,),
            in_specs=[held] * (len(xs) + 2 + len(prior)),
            out_specs=held,
            scratch_shapes=[
                pltpu.VMEM((R1, spectra * inputs, 2 * R2), jnp.float32),
                pltpu.VMEM((spectra, F, LANES), jnp.float32),
            ],
        ),
        compiler_params=pltpu.CompilerParams(vmem_limit_bytes=CHANNEL_VMEM),
        cost_estimate=pl.CostEstimate(flops=10**9 * spectra, bytes_accessed=8 * 2**20, transcendentals=0),
        name="channels",
    )(first, *xs, rows_table, table, *prior)


def correlate_kernel(n_tim, mixed, scale, valid_ref, piece, *refs):
    if len(refs) == 6:
        partial_hbm, out, rows_k, rows_i, partial, arrived = refs
        fetch = [pltpu.make_async_copy(partial_hbm.at[k], partial.at[k], arrived.at[k]) for k in range(CAP)]
    else:
        out, rows_k, rows_i = refs
        partial = fetch = None
    slot, block = pl.program_id(0), pl.program_id(1)
    depth, width = rows_k.shape[1], rows_k.shape[2]
    held = partial is None
    tile = TILE
    blocks = width // tile
    half = depth // 2

    def arrange(which, q):
        lane = lax.broadcasted_iota(jnp.int32, (2 * AVG, LANES), 1)
        low, lower = lane < LANES // 2, lane % (LANES // 2) < LANES // 4
        lanes = pl.ds(pl.multiple_of(q * LANES, LANES), LANES)

        base = 0
        for u in range(n_tim // 2):
            group = [
                [piece[(2 * q + e) * n_tim + 2 * u + v, which].astype(jnp.float32) for v in range(2)]
                for e in range(2)
            ]
            if mixed:
                for e in range(2):
                    for v in range(2):
                        later = (2 * u + v + 1) % n_tim
                        other = piece[(2 * q + e) * n_tim + later, which].astype(jnp.float32)[AVG:]
                        mine = group[e][v]
                        turn = jnp.where(lower[:AVG], other, mine[AVG:])
                        group[e][v] = jnp.concatenate([mine[:AVG], turn], axis=0)
            for s in range(piece.shape[2] // AVG):
                even, odd = [
                    jnp.concatenate([group[e][v][AVG * s : AVG * s + AVG] for v in range(2)], axis=0)
                    for e in range(2)
                ]
                re = jnp.where(low, even, pltpu.roll(odd, LANES // 2, 1))
                im = jnp.where(low, pltpu.roll(even, LANES // 2, 1), odd)
                rows_k[which, base : base + 2 * AVG, lanes] = re.astype(jnp.bfloat16)
                rows_k[which, half + base : half + base + 2 * AVG, lanes] = im.astype(jnp.bfloat16)
                base += 2 * AVG
        turned = rows_k[which, :, lanes].T
        rows_i[which, lanes, :depth] = turned
        rows_i[which, lanes, depth:] = -turned[:, :half]

    @pl.when(jnp.logical_and(slot == 0, block == 0))
    def _():
        if fetch is not None:
            for copy in fetch:
                copy.start()
        lax.fori_loop(0, width // LANES, lambda q, carry: (arrange(0, q), carry)[1], 0)

    if fetch is not None:
        for which in range(CAP):
            pl.when(jnp.logical_and(slot == which, block == 0))(fetch[which].wait)

    def strip(which, i):
        upper = lax.broadcasted_iota(jnp.int32, (tile, tile), 0) <= lax.broadcasted_iota(
            jnp.int32, (tile, tile), 1
        )
        keep = valid_ref[which] != 0
        rows = slice(i * tile, (i + 1) * tile)
        for j in range(blocks):
            lanes = slice(j * tile, (j + 1) * tile)
            other = rows_k[which, :, lanes]
            real = imag = None
            if i <= j:
                real = jnp.dot(rows_i[which, rows, :depth], other, preferred_element_type=jnp.float32)
            if i >= j:
                imag = jnp.dot(rows_i[which, rows, half:], other, preferred_element_type=jnp.float32)
            value = real if imag is None else imag if real is None else jnp.where(upper, real, imag)
            if partial is not None:
                value = value + partial[which, rows, lanes].astype(jnp.float32)
            value = jnp.where(keep, value * scale, 0.0)
            if held:
                out[which, rows, lanes] = value.astype(out.dtype)
            else:
                out[0, :, lanes] = value

    each = width // LANES // blocks
    for which in range(CAP):
        for i in range(blocks):

            @pl.when(jnp.logical_and(slot == which, block == i))
            def _():
                if which + 1 < CAP:
                    for q in range(each):
                        arrange(which + 1, i * each + q)
                strip(which, i)


def correlate_call(n_inp, n_tim, mixed, scale, valid, piece, partial=None):
    width = n_inp * LANES // 2
    depth = n_tim * piece.shape[2] * 2
    tile = TILE
    block = pl.BlockSpec((1, tile, width), lambda s, i, *_: (s, i, 0))
    held = pl.BlockSpec(memory_space=pltpu.VMEM)
    more = [] if partial is None else [partial]
    return pl.pallas_call(
        functools.partial(correlate_kernel, n_tim, mixed, scale),
        out_shape=jax.ShapeDtypeStruct((CAP, width, width), jnp.float32 if more else jnp.bfloat16),
        grid_spec=pltpu.PrefetchScalarGridSpec(
            num_scalar_prefetch=1,
            grid=(CAP, width // tile),
            in_specs=[held] + [pl.BlockSpec(memory_space=pl.ANY)] * len(more),
            out_specs=block if more else held,
            scratch_shapes=[
                pltpu.VMEM((CAP, depth, width), jnp.bfloat16),
                pltpu.VMEM((CAP, width, depth + depth // 2), jnp.bfloat16),
            ]
            + [pltpu.VMEM(p.shape, p.dtype) for p in more]
            + [pltpu.SemaphoreType.DMA((CAP,)) for _ in more],
        ),
        compiler_params=pltpu.CompilerParams(vmem_limit_bytes=CORRELATE_VMEM),
        cost_estimate=pl.CostEstimate(flops=5 * 10**9, bytes_accessed=19 * 2**20, transcendentals=0),
        name="correlate",
    )(valid, piece, *more)


def body(voltages, scale_exps, owner_table):
    n_inp = lax.axis_size("inp")
    n_tim = lax.axis_size("tim")
    devices = n_inp * n_tim
    spec_dev = voltages.shape[2] // F
    *own, low2, high1 = sample_call(voltages, scale_exps)
    ahead = [(source, source + 1) for source in range(n_tim - 1)]
    back = [(source, (source - 1) % n_tim) for source in range(n_tim)]
    half = voltages.shape[1] // 2
    minus1 = lax.ppermute(own[3], "tim", ahead)
    plus0 = lax.ppermute(own[0], "tim", back)
    minus2 = lax.ppermute(low2, "tim", ahead)
    plus1 = lax.ppermute(high1, "tim", back)

    rows = owner_rows(owner_table, CAP)
    match = rows[None, :] == jnp.arange(devices * CAP, dtype=jnp.int32)[:, None]
    valid = jnp.any(match, axis=1).astype(jnp.int32)
    which = jnp.sum(jnp.where(match, jnp.arange(CH, dtype=jnp.int32)[None, :], 0), axis=1)
    first = (which * AVG - AVG * CH // 2) % F
    me = lax.axis_index("inp") * n_tim + lax.axis_index("tim")
    mine = lax.dynamic_slice(valid, (me * CAP,), (CAP,))

    table = jnp.asarray(radix_table()).astype(jnp.bfloat16)

    last = (lax.axis_index("tim") == n_tim - 1).astype(jnp.int32)
    first = jnp.concatenate([first, last[None]])
    tables = (jnp.asarray(row_table()), table)
    x0, x1, x2, x3 = [(s, 0) for s in range(spec_dev)]
    third = channel_call([[((x0, x1, x2, x3), 0)]], first, own, *tables)
    near = channel_call([[(((3, 0), x0, x1, x2), 0)]], first, (*own[:3], minus1), *tables, prior=(third,))
    near, plus0, minus2, plus1 = lax.optimization_barrier((near, plus0, minus2, plus1))
    near = lax.all_to_all(near, ("inp", "tim"), split_axis=0, concat_axis=0, tiled=True)
    m1, m2, p0, p1 = (4, 0), (5, 0), (6, 0), (7, half)
    plan = [[((x1, x2, x3, p0), 3)], [((m2, m1, x0, x1), 0), ((x2, x3, p0, p1), 2)]]
    far = channel_call(plan, first, (*own, minus1, minus2, plus0, plus1), *tables)
    far = lax.all_to_all(far, ("inp", "tim"), split_axis=0, concat_axis=0, tiled=True)
    partial = correlate_call(n_inp, n_tim, False, 1.0, mine, near)
    return correlate_call(n_inp, n_tim, True, 1.0 / (n_tim * spec_dev * AVG), mine, far, partial)


def solution(mesh):
    return jax.shard_map(
        body,
        mesh=mesh,
        in_specs=(P(None, "inp", "tim"), P("inp", "tim"), P()),
        out_specs=P(("inp", "tim"), None, None),
        check_vma=False,
    )
```

```python
import functools
import math

import jax
import jax.numpy as jnp
import numpy as np
from jax import lax
from jax.experimental import pallas as pl
from jax.experimental.pallas import tpu as pltpu
from jax.sharding import PartitionSpec as P

F = 4096
AVG = 24
CH = 144
TAPS = 4
CAP = 2
R1 = 16
R2 = 256
LANES = 128
SAMPLE_VMEM = 46 * 2**20
CHANNEL_VMEM = 30 * 2**20
CORRELATE_VMEM = 50 * 2**20
TILE = 256


def row_table():
    length = TAPS * F
    steps = np.arange(length, dtype=np.float64)
    centre = (steps + 0.5 - length / 2.0) / F
    taper = 0.5 - 0.5 * np.cos(2.0 * math.pi * (steps + 0.5) / length)
    taps = (np.sinc(centre) * taper).reshape(TAPS, F)
    angle = 2.0 * math.pi * (np.arange(R1)[:, None] * np.arange(R2)[None, :]).reshape(1, F) / F
    rows = [taps, np.cos(angle) / math.sqrt(F), np.sin(angle) / math.sqrt(F), np.zeros((2, F))]
    return np.concatenate(rows, axis=0).astype(np.float32)


def radix_table():
    phase = np.arange(R2)[:, None] * np.arange(R2)[None, :] % R2
    angle = 2.0 * math.pi * phase / R2
    cosine, sine = np.cos(angle), np.sin(angle)
    table = np.concatenate(
        [np.concatenate([cosine, sine], axis=1), np.concatenate([-sine, cosine], axis=1)], axis=0
    )
    return table.astype(np.float32)


def owner_rows(owner_table, cap):
    index = jnp.arange(owner_table.shape[0], dtype=jnp.int32)
    same = owner_table[:, None] == owner_table[None, :]
    earlier = index[None, :] < index[:, None]
    slot = jnp.sum((same & earlier).astype(jnp.int32), axis=1)
    return owner_table * cap + slot


def four(a, b, c, d):
    sr, si = a[0] + c[0], a[1] + c[1]
    tr, ti = a[0] - c[0], a[1] - c[1]
    ur, ui = b[0] + d[0], b[1] + d[1]
    vr, vi = b[0] - d[0], b[1] - d[1]
    return (sr + ur, si + ui), (tr + vi, ti - vr), (sr - ur, si - ui), (tr - vi, ti + vr)


def turn(value, power):
    re, im = value
    power %= 16
    if power == 0:
        return value
    if power == 4:
        return im, -re
    root = math.sqrt(0.5)
    if power == 2:
        return (re + im) * root, (im - re) * root
    if power == 6:
        return (im - re) * root, (re + im) * (-root)
    cosine, sine = math.cos(2 * math.pi * power / 16), math.sin(2 * math.pi * power / 16)
    return re * cosine + im * sine, im * cosine - re * sine


def sixteen(x):
    inner = [four(x[b], x[4 + b], x[8 + b], x[12 + b]) for b in range(4)]
    out = [None] * 16
    for c in range(4):
        row = four(*[turn(inner[b][c], b * c) for b in range(4)])
        for d in range(4):
            out[c + 4 * d] = row[d]
    return out


def sample_kernel(first, count, exps, voltages, *outs):
    wholes, halves = outs[:count], outs[count:]
    step, block = pl.program_id(0), voltages.shape[1]
    rows = pl.ds(pl.multiple_of(step * block, block), block)
    factor = jnp.left_shift(1, exps[rows, :]).astype(jnp.float32) * (1.0 / 128.0)
    for k, whole in enumerate(wholes):
        s = first + k
        for c in range(2):
            value = voltages[c, :, k * F : (k + 1) * F].astype(jnp.float32) * factor[:, s : s + 1]
            value = value.astype(jnp.bfloat16)
            whole[c, rows, :] = value
            if halves and s == 2:

                @pl.when(step * block < halves[0].shape[1])
                def _():
                    halves[0][c, rows, :] = value

            if halves and s == 1:
                half = halves[1].shape[1]

                @pl.when(step * block >= half)
                def _():
                    halves[1][c, pl.ds(pl.multiple_of(step * block - half, block), block), :] = value


def sample_call(voltages, exps, first, count, halves):
    inputs = exps.shape[0]
    block = 16
    held = pl.BlockSpec(memory_space=pltpu.VMEM)
    shapes = [(2, inputs, F)] * count + [(2, inputs // 2, F)] * (2 if halves else 0)
    return pl.pallas_call(
        functools.partial(sample_kernel, first, count),
        out_shape=[jax.ShapeDtypeStruct(shape, jnp.bfloat16) for shape in shapes],
        grid=(inputs // block,),
        in_specs=[held, pl.BlockSpec((2, block, count * F), lambda i: (0, i, first // count))],
        out_specs=[held] * len(shapes),
        compiler_params=pltpu.CompilerParams(vmem_limit_bytes=SAMPLE_VMEM),
        cost_estimate=pl.CostEstimate(
            flops=10**7, bytes_accessed=(3 * count + len(shapes) - count) * 2**20, transcendentals=0
        ),
        name="samples",
    )(exps, voltages)


def channel_kernel(plan, count, first_ref, *refs):
    xs, (rows_table, table) = refs[:count], refs[count : count + 2]
    prior, (out, turned, spectrum) = refs[count + 2 : -3], refs[-3:]
    step = pl.program_id(0)
    spectra = len(plan)
    block = 16
    inputs = turned.shape[1] // spectra
    slots = out.shape[0] * out.shape[1]
    wrapped = first_ref[slots] != 0

    def columns(s, blocks, cut, half):
        base = half * LANES
        lanes2 = pl.ds(pl.multiple_of(base, LANES), LANES)
        lanes3 = pl.ds(pl.multiple_of(base + R2, LANES), LANES)
        for r in range(block // 8):
            series = []
            for n in range(R1):
                lanes = pl.ds(pl.multiple_of(base + n * R2, LANES), LANES)
                parts = []
                for c in range(2):
                    total = None
                    for tap in range(TAPS):
                        index, skip = blocks[tap]
                        members = pl.ds(pl.multiple_of(step * block - skip, block), block)
                        value = xs[index][c, members, lanes].astype(jnp.float32)[8 * r : 8 * r + 8]
                        weight = rows_table[tap : tap + 1, lanes]
                        if tap < cut:
                            weight = jnp.where(wrapped, 0.0, weight)
                        term = weight * value
                        total = term if total is None else total + term
                    parts.append(total.astype(jnp.bfloat16).astype(jnp.float32))
                series.append(tuple(parts))
            result = sixteen(series)
            row = pl.ds(pl.multiple_of(step * block + s * inputs + 8 * r, 8), 8)
            for m in range(R1):
                re, im = result[m]
                lanes = pl.ds(pl.multiple_of(base + m * R2, LANES), LANES)
                cosine, sine = [rows_table[TAPS + k : TAPS + 1 + k, lanes] for k in range(2)]
                turned[m, row, lanes2] = re * cosine + im * sine
                turned[m, row, lanes3] = im * cosine - re * sine

    def filtered(s, blocks, cut):
        lax.fori_loop(0, R2 // LANES, lambda half, carry: (columns(s, blocks, cut, half), carry)[1], 0)

    middle = pl.num_programs(0) // 2
    for s, options in enumerate(plan):
        if len(options) == 1:
            filtered(s, *options[0])
        else:
            pl.when(step < middle)(functools.partial(filtered, s, *options[0]))
            pl.when(step >= middle)(functools.partial(filtered, s, *options[1]))

    @pl.when(step == pl.num_programs(0) - 1)
    def _():
        weights = table[...]
        low = lax.broadcasted_iota(jnp.int32, (R2, LANES), 1) < LANES // 2
        many = 4
        for m in range(0, R1, many):
            rows = turned[m : m + many].reshape(many * spectra * inputs, 2 * R2).astype(jnp.bfloat16)
            result = lax.dot_general(
                weights, rows, (((1,), (1,)), ((), ())), preferred_element_type=jnp.float32
            )
            for tile in range(many * spectra // 2):
                lanes = slice(tile * LANES, (tile + 1) * LANES)
                re, im = result[:R2, lanes], result[R2:, lanes]
                pair = (
                    jnp.where(low, re, pltpu.roll(im, LANES // 2, 1)),
                    jnp.where(low, pltpu.roll(re, LANES // 2, 1), im),
                )
                for e in range(2):
                    more, s = divmod(2 * tile + e, spectra)
                    spectrum[s, pl.ds(m + more, R2, stride=R1), :] = pair[e]

        def place(owner, carry):
            for slot in range(CAP):
                start = pl.multiple_of(first_ref[owner * CAP + slot], 8)
                rows = [p[owner, slot].astype(jnp.float32) for p in prior]
                rows += [spectrum[s, pl.ds(start, AVG), :] for s in range(spectra)]
                rows = rows[0] if len(rows) == 1 else jnp.concatenate(rows, axis=0)
                out[owner, slot] = rows.astype(jnp.bfloat16)
            return carry

        lax.fori_loop(0, out.shape[0], place, 0, unroll=2)


def channel_call(plan, first, xs, rows_table, table, prior=()):
    owners = (first.shape[0] - 1) // CAP
    block = 16
    inputs = xs[0].shape[1]
    spectra = len(plan)
    held = pl.BlockSpec(memory_space=pltpu.VMEM)
    shape = (owners, CAP, (spectra + len(prior)) * AVG, LANES)
    return pl.pallas_call(
        functools.partial(channel_kernel, plan, len(xs)),
        out_shape=jax.ShapeDtypeStruct(shape, jnp.bfloat16),
        grid_spec=pltpu.PrefetchScalarGridSpec(
            num_scalar_prefetch=1,
            grid=(inputs // block,),
            in_specs=[held] * (len(xs) + 2 + len(prior)),
            out_specs=held,
            scratch_shapes=[
                pltpu.VMEM((R1, spectra * inputs, 2 * R2), jnp.float32),
                pltpu.VMEM((spectra, F, LANES), jnp.float32),
            ],
        ),
        compiler_params=pltpu.CompilerParams(vmem_limit_bytes=CHANNEL_VMEM),
        cost_estimate=pl.CostEstimate(flops=10**9 * spectra, bytes_accessed=8 * 2**20, transcendentals=0),
        name="channels",
    )(first, *xs, rows_table, table, *prior)


def correlate_kernel(n_tim, mixed, scale, valid_ref, piece, *refs):
    if len(refs) == 6:
        partial_hbm, out, rows_k, rows_i, partial, arrived = refs
        fetch = [pltpu.make_async_copy(partial_hbm.at[k], partial.at[k], arrived.at[k]) for k in range(CAP)]
    else:
        out, rows_k, rows_i = refs
        partial = fetch = None
    slot, block = pl.program_id(0), pl.program_id(1)
    depth, width = rows_k.shape[1], rows_k.shape[2]
    held = partial is None
    tile = TILE
    blocks = width // tile
    half = depth // 2

    def arrange(which, q):
        lane = lax.broadcasted_iota(jnp.int32, (2 * AVG, LANES), 1)
        low, lower = lane < LANES // 2, lane % (LANES // 2) < LANES // 4
        lanes = pl.ds(pl.multiple_of(q * LANES, LANES), LANES)

        base = 0
        for u in range(n_tim // 2):
            group = [
                [piece[(2 * q + e) * n_tim + 2 * u + v, which].astype(jnp.float32) for v in range(2)]
                for e in range(2)
            ]
            if mixed:
                for e in range(2):
                    for v in range(2):
                        later = (2 * u + v + 1) % n_tim
                        other = piece[(2 * q + e) * n_tim + later, which].astype(jnp.float32)[AVG:]
                        mine = group[e][v]
                        turn = jnp.where(lower[:AVG], other, mine[AVG:])
                        group[e][v] = jnp.concatenate([mine[:AVG], turn], axis=0)
            for s in range(piece.shape[2] // AVG):
                even, odd = [
                    jnp.concatenate([group[e][v][AVG * s : AVG * s + AVG] for v in range(2)], axis=0)
                    for e in range(2)
                ]
                re = jnp.where(low, even, pltpu.roll(odd, LANES // 2, 1))
                im = jnp.where(low, pltpu.roll(even, LANES // 2, 1), odd)
                rows_k[which, base : base + 2 * AVG, lanes] = re.astype(jnp.bfloat16)
                rows_k[which, half + base : half + base + 2 * AVG, lanes] = im.astype(jnp.bfloat16)
                base += 2 * AVG
        turned = rows_k[which, :, lanes].T
        rows_i[which, lanes, :depth] = turned
        rows_i[which, lanes, depth:] = -turned[:, :half]

    @pl.when(jnp.logical_and(slot == 0, block == 0))
    def _():
        if fetch is not None:
            for copy in fetch:
                copy.start()
        lax.fori_loop(0, width // LANES, lambda q, carry: (arrange(0, q), carry)[1], 0)

    if fetch is not None:
        for which in range(CAP):
            pl.when(jnp.logical_and(slot == which, block == 0))(fetch[which].wait)

    def strip(which, i):
        upper = lax.broadcasted_iota(jnp.int32, (tile, tile), 0) <= lax.broadcasted_iota(
            jnp.int32, (tile, tile), 1
        )
        keep = valid_ref[which] != 0
        rows = slice(i * tile, (i + 1) * tile)
        for j in range(blocks):
            lanes = slice(j * tile, (j + 1) * tile)
            other = rows_k[which, :, lanes]
            real = imag = None
            if i <= j:
                real = jnp.dot(rows_i[which, rows, :depth], other, preferred_element_type=jnp.float32)
            if i >= j:
                imag = jnp.dot(rows_i[which, rows, half:], other, preferred_element_type=jnp.float32)
            value = real if imag is None else imag if real is None else jnp.where(upper, real, imag)
            if partial is not None:
                value = value + partial[which, rows, lanes].astype(jnp.float32)
            value = jnp.where(keep, value * scale, 0.0)
            if held:
                out[which, rows, lanes] = value.astype(out.dtype)
            else:
                out[0, :, lanes] = value

    each = width // LANES // blocks
    for which in range(CAP):
        for i in range(blocks):

            @pl.when(jnp.logical_and(slot == which, block == i))
            def _():
                if which + 1 < CAP:
                    for q in range(each):
                        arrange(which + 1, i * each + q)
                strip(which, i)


def correlate_call(n_inp, n_tim, mixed, scale, valid, piece, partial=None):
    width = n_inp * LANES // 2
    depth = n_tim * piece.shape[2] * 2
    tile = TILE
    block = pl.BlockSpec((1, tile, width), lambda s, i, *_: (s, i, 0))
    held = pl.BlockSpec(memory_space=pltpu.VMEM)
    more = [] if partial is None else [partial]
    return pl.pallas_call(
        functools.partial(correlate_kernel, n_tim, mixed, scale),
        out_shape=jax.ShapeDtypeStruct((CAP, width, width), jnp.float32 if more else jnp.bfloat16),
        grid_spec=pltpu.PrefetchScalarGridSpec(
            num_scalar_prefetch=1,
            grid=(CAP, width // tile),
            in_specs=[held] + [pl.BlockSpec(memory_space=pl.ANY)] * len(more),
            out_specs=block if more else held,
            scratch_shapes=[
                pltpu.VMEM((CAP, depth, width), jnp.bfloat16),
                pltpu.VMEM((CAP, width, depth + depth // 2), jnp.bfloat16),
            ]
            + [pltpu.VMEM(p.shape, p.dtype) for p in more]
            + [pltpu.SemaphoreType.DMA((CAP,)) for _ in more],
        ),
        compiler_params=pltpu.CompilerParams(vmem_limit_bytes=CORRELATE_VMEM),
        cost_estimate=pl.CostEstimate(flops=5 * 10**9, bytes_accessed=19 * 2**20, transcendentals=0),
        name="correlate",
    )(valid, piece, *more)


def body(voltages, scale_exps, owner_table):
    n_inp = lax.axis_size("inp")
    n_tim = lax.axis_size("tim")
    devices = n_inp * n_tim
    spec_dev = voltages.shape[2] // F
    (last_own,) = sample_call(voltages, scale_exps, spec_dev - 1, 1, False)
    last_own, held_back = lax.optimization_barrier((last_own, voltages))
    *own, low2, high1 = sample_call(held_back, scale_exps, 0, spec_dev - 1, True)
    own.append(last_own)
    ahead = [(source, source + 1) for source in range(n_tim - 1)]
    back = [(source, (source - 1) % n_tim) for source in range(n_tim)]
    half = voltages.shape[1] // 2
    minus1 = lax.ppermute(own[3], "tim", ahead)
    plus0 = lax.ppermute(own[0], "tim", back)
    minus2 = lax.ppermute(low2, "tim", ahead)
    plus1 = lax.ppermute(high1, "tim", back)

    rows = owner_rows(owner_table, CAP)
    match = rows[None, :] == jnp.arange(devices * CAP, dtype=jnp.int32)[:, None]
    valid = jnp.any(match, axis=1).astype(jnp.int32)
    which = jnp.sum(jnp.where(match, jnp.arange(CH, dtype=jnp.int32)[None, :], 0), axis=1)
    first = (which * AVG - AVG * CH // 2) % F
    me = lax.axis_index("inp") * n_tim + lax.axis_index("tim")
    mine = lax.dynamic_slice(valid, (me * CAP,), (CAP,))

    table = jnp.asarray(radix_table()).astype(jnp.bfloat16)

    last = (lax.axis_index("tim") == n_tim - 1).astype(jnp.int32)
    first = jnp.concatenate([first, last[None]])
    tables = (jnp.asarray(row_table()), table)
    x0, x1, x2, x3 = [(s, 0) for s in range(spec_dev)]
    third = channel_call([[((x0, x1, x2, x3), 0)]], first, own, *tables)
    near = channel_call([[(((3, 0), x0, x1, x2), 0)]], first, (*own[:3], minus1), *tables, prior=(third,))
    near, plus0, minus2, plus1 = lax.optimization_barrier((near, plus0, minus2, plus1))
    near = lax.all_to_all(near, ("inp", "tim"), split_axis=0, concat_axis=0, tiled=True)
    m1, m2, p0, p1 = (4, 0), (5, 0), (6, 0), (7, half)
    plan = [[((x1, x2, x3, p0), 3)], [((m2, m1, x0, x1), 0), ((x2, x3, p0, p1), 2)]]
    far = channel_call(plan, first, (*own, minus1, minus2, plus0, plus1), *tables)
    far = lax.all_to_all(far, ("inp", "tim"), split_axis=0, concat_axis=0, tiled=True)
    partial = correlate_call(n_inp, n_tim, False, 1.0, mine, near)
    return correlate_call(n_inp, n_tim, True, 1.0 / (n_tim * spec_dev * AVG), mine, far, partial)


def solution(mesh):
    return jax.shard_map(
        body,
        mesh=mesh,
        in_specs=(P(None, "inp", "tim"), P("inp", "tim"), P()),
        out_specs=P(("inp", "tim"), None, None),
        check_vma=False,
    )
```

```python
import functools
import math

import jax
import jax.numpy as jnp
import numpy as np
from jax import lax
from jax.experimental import pallas as pl
from jax.experimental.pallas import tpu as pltpu
from jax.sharding import PartitionSpec as P

F = 4096
AVG = 24
CH = 144
TAPS = 4
CAP = 2
R1 = 16
R2 = 256
LANES = 128
SAMPLE_VMEM = 46 * 2**20
CHANNEL_VMEM = 30 * 2**20
CORRELATE_VMEM = 50 * 2**20
TILE = 256


def row_table():
    length = TAPS * F
    steps = np.arange(length, dtype=np.float64)
    centre = (steps + 0.5 - length / 2.0) / F
    taper = 0.5 - 0.5 * np.cos(2.0 * math.pi * (steps + 0.5) / length)
    taps = (np.sinc(centre) * taper).reshape(TAPS, F)
    angle = 2.0 * math.pi * (np.arange(R1)[:, None] * np.arange(R2)[None, :]).reshape(1, F) / F
    rows = [taps, np.cos(angle) / math.sqrt(F), np.sin(angle) / math.sqrt(F), np.zeros((2, F))]
    return np.concatenate(rows, axis=0).astype(np.float32)


def radix_table():
    phase = np.arange(R2)[:, None] * np.arange(R2)[None, :] % R2
    angle = 2.0 * math.pi * phase / R2
    cosine, sine = np.cos(angle), np.sin(angle)
    table = np.concatenate(
        [np.concatenate([cosine, sine], axis=1), np.concatenate([-sine, cosine], axis=1)], axis=0
    )
    return table.astype(np.float32)


def owner_rows(owner_table, cap):
    index = jnp.arange(owner_table.shape[0], dtype=jnp.int32)
    same = owner_table[:, None] == owner_table[None, :]
    earlier = index[None, :] < index[:, None]
    slot = jnp.sum((same & earlier).astype(jnp.int32), axis=1)
    return owner_table * cap + slot


def four(a, b, c, d):
    sr, si = a[0] + c[0], a[1] + c[1]
    tr, ti = a[0] - c[0], a[1] - c[1]
    ur, ui = b[0] + d[0], b[1] + d[1]
    vr, vi = b[0] - d[0], b[1] - d[1]
    return (sr + ur, si + ui), (tr + vi, ti - vr), (sr - ur, si - ui), (tr - vi, ti + vr)


def turn(value, power):
    re, im = value
    power %= 16
    if power == 0:
        return value
    if power == 4:
        return im, -re
    root = math.sqrt(0.5)
    if power == 2:
        return (re + im) * root, (im - re) * root
    if power == 6:
        return (im - re) * root, (re + im) * (-root)
    cosine, sine = math.cos(2 * math.pi * power / 16), math.sin(2 * math.pi * power / 16)
    return re * cosine + im * sine, im * cosine - re * sine


def sixteen(x):
    inner = [four(x[b], x[4 + b], x[8 + b], x[12 + b]) for b in range(4)]
    out = [None] * 16
    for c in range(4):
        row = four(*[turn(inner[b][c], b * c) for b in range(4)])
        for d in range(4):
            out[c + 4 * d] = row[d]
    return out


def sample_kernel(exps, voltages, *outs):
    wholes, low2, high1 = outs[:-2], outs[-2], outs[-1]
    step, block = pl.program_id(0), voltages.shape[1]
    half = low2.shape[1]
    rows = pl.ds(pl.multiple_of(step * block, block), block)
    factor = jnp.left_shift(1, exps[rows, :]).astype(jnp.float32) * (1.0 / 128.0)
    each = voltages.shape[2] // F

    def make(s):
        k = s % each
        for c in range(2):
            value = voltages[c, :, k * F : (k + 1) * F].astype(jnp.float32) * factor[:, s : s + 1]
            value = value.astype(jnp.bfloat16)
            wholes[s][c, rows, :] = value
            if s == 2:

                @pl.when(step * block < half)
                def _():
                    low2[c, rows, :] = value

            if s == 1:

                @pl.when(step * block >= half)
                def _():
                    high1[c, pl.ds(pl.multiple_of(step * block - half, block), block), :] = value

    for part in range(len(wholes) // each):

        @pl.when(pl.program_id(1) == part)
        def _():
            for k in range(each):
                make(part * each + k)


def sample_call(voltages, exps):
    inputs, spectra = exps.shape
    block = 16
    held = pl.BlockSpec(memory_space=pltpu.VMEM)
    shapes = [(2, inputs, F)] * spectra + [(2, inputs // 2, F)] * 2
    return pl.pallas_call(
        sample_kernel,
        out_shape=[jax.ShapeDtypeStruct(shape, jnp.bfloat16) for shape in shapes],
        grid=(inputs // block, spectra),
        in_specs=[held, pl.BlockSpec((2, block, F), lambda i, h: (0, i, h))],
        out_specs=[held] * len(shapes),
        compiler_params=pltpu.CompilerParams(vmem_limit_bytes=SAMPLE_VMEM),
        cost_estimate=pl.CostEstimate(flops=10**7, bytes_accessed=13 * 2**20, transcendentals=0),
        name="samples",
    )(exps, voltages)


def channel_kernel(plan, count, first_ref, *refs):
    xs, (rows_table, table) = refs[:count], refs[count : count + 2]
    prior, (out, turned, spectrum) = refs[count + 2 : -3], refs[-3:]
    step = pl.program_id(0)
    spectra = len(plan)
    block = 16
    inputs = turned.shape[1] // spectra
    slots = out.shape[0] * out.shape[1]
    wrapped = first_ref[slots] != 0

    def columns(s, blocks, cut, half):
        base = half * LANES
        lanes2 = pl.ds(pl.multiple_of(base, LANES), LANES)
        lanes3 = pl.ds(pl.multiple_of(base + R2, LANES), LANES)
        for r in range(block // 8):
            series = []
            for n in range(R1):
                lanes = pl.ds(pl.multiple_of(base + n * R2, LANES), LANES)
                parts = []
                for c in range(2):
                    total = None
                    for tap in range(TAPS):
                        index, skip = blocks[tap]
                        members = pl.ds(pl.multiple_of(step * block - skip, block), block)
                        value = xs[index][c, members, lanes].astype(jnp.float32)[8 * r : 8 * r + 8]
                        weight = rows_table[tap : tap + 1, lanes]
                        if tap < cut:
                            weight = jnp.where(wrapped, 0.0, weight)
                        term = weight * value
                        total = term if total is None else total + term
                    parts.append(total.astype(jnp.bfloat16).astype(jnp.float32))
                series.append(tuple(parts))
            result = sixteen(series)
            row = pl.ds(pl.multiple_of(step * block + s * inputs + 8 * r, 8), 8)
            for m in range(R1):
                re, im = result[m]
                lanes = pl.ds(pl.multiple_of(base + m * R2, LANES), LANES)
                cosine, sine = [rows_table[TAPS + k : TAPS + 1 + k, lanes] for k in range(2)]
                turned[m, row, lanes2] = re * cosine + im * sine
                turned[m, row, lanes3] = im * cosine - re * sine

    def filtered(s, blocks, cut):
        lax.fori_loop(0, R2 // LANES, lambda half, carry: (columns(s, blocks, cut, half), carry)[1], 0)

    middle = pl.num_programs(0) // 2
    for s, options in enumerate(plan):
        if len(options) == 1:
            filtered(s, *options[0])
        else:
            pl.when(step < middle)(functools.partial(filtered, s, *options[0]))
            pl.when(step >= middle)(functools.partial(filtered, s, *options[1]))

    @pl.when(step == pl.num_programs(0) - 1)
    def _():
        weights = table[...]
        low = lax.broadcasted_iota(jnp.int32, (R2, LANES), 1) < LANES // 2
        many = 4
        for m in range(0, R1, many):
            rows = turned[m : m + many].reshape(many * spectra * inputs, 2 * R2).astype(jnp.bfloat16)
            result = lax.dot_general(
                weights, rows, (((1,), (1,)), ((), ())), preferred_element_type=jnp.float32
            )
            for tile in range(many * spectra // 2):
                lanes = slice(tile * LANES, (tile + 1) * LANES)
                re, im = result[:R2, lanes], result[R2:, lanes]
                pair = (
                    jnp.where(low, re, pltpu.roll(im, LANES // 2, 1)),
                    jnp.where(low, pltpu.roll(re, LANES // 2, 1), im),
                )
                for e in range(2):
                    more, s = divmod(2 * tile + e, spectra)
                    spectrum[s, pl.ds(m + more, R2, stride=R1), :] = pair[e]

        def place(owner, carry):
            for slot in range(CAP):
                start = pl.multiple_of(first_ref[owner * CAP + slot], 8)
                rows = [p[owner, slot].astype(jnp.float32) for p in prior]
                rows += [spectrum[s, pl.ds(start, AVG), :] for s in range(spectra)]
                rows = rows[0] if len(rows) == 1 else jnp.concatenate(rows, axis=0)
                out[owner, slot] = rows.astype(jnp.bfloat16)
            return carry

        lax.fori_loop(0, out.shape[0], place, 0, unroll=2)


def channel_call(plan, first, xs, rows_table, table, prior=()):
    owners = (first.shape[0] - 1) // CAP
    block = 16
    inputs = xs[0].shape[1]
    spectra = len(plan)
    held = pl.BlockSpec(memory_space=pltpu.VMEM)
    shape = (owners, CAP, (spectra + len(prior)) * AVG, LANES)
    return pl.pallas_call(
        functools.partial(channel_kernel, plan, len(xs)),
        out_shape=jax.ShapeDtypeStruct(shape, jnp.bfloat16),
        grid_spec=pltpu.PrefetchScalarGridSpec(
            num_scalar_prefetch=1,
            grid=(inputs // block,),
            in_specs=[held] * (len(xs) + 2 + len(prior)),
            out_specs=held,
            scratch_shapes=[
                pltpu.VMEM((R1, spectra * inputs, 2 * R2), jnp.float32),
                pltpu.VMEM((spectra, F, LANES), jnp.float32),
            ],
        ),
        compiler_params=pltpu.CompilerParams(vmem_limit_bytes=CHANNEL_VMEM),
        cost_estimate=pl.CostEstimate(flops=10**9 * spectra, bytes_accessed=8 * 2**20, transcendentals=0),
        name="channels",
    )(first, *xs, rows_table, table, *prior)


def correlate_kernel(n_tim, mixed, scale, valid_ref, piece, *refs):
    if len(refs) == 6:
        partial_hbm, out, rows_k, rows_i, partial, arrived = refs
        fetch = [pltpu.make_async_copy(partial_hbm.at[k], partial.at[k], arrived.at[k]) for k in range(CAP)]
    else:
        out, rows_k, rows_i = refs
        partial = fetch = None
    slot, block = pl.program_id(0), pl.program_id(1)
    depth, width = rows_k.shape[1], rows_k.shape[2]
    held = partial is None
    tile = TILE
    blocks = width // tile
    half = depth // 2

    def arrange(which, q):
        lane = lax.broadcasted_iota(jnp.int32, (2 * AVG, LANES), 1)
        low, lower = lane < LANES // 2, lane % (LANES // 2) < LANES // 4
        lanes = pl.ds(pl.multiple_of(q * LANES, LANES), LANES)

        base = 0
        for u in range(n_tim // 2):
            group = [
                [piece[(2 * q + e) * n_tim + 2 * u + v, which].astype(jnp.float32) for v in range(2)]
                for e in range(2)
            ]
            if mixed:
                for e in range(2):
                    for v in range(2):
                        later = (2 * u + v + 1) % n_tim
                        other = piece[(2 * q + e) * n_tim + later, which].astype(jnp.float32)[AVG:]
                        mine = group[e][v]
                        turn = jnp.where(lower[:AVG], other, mine[AVG:])
                        group[e][v] = jnp.concatenate([mine[:AVG], turn], axis=0)
            for s in range(piece.shape[2] // AVG):
                even, odd = [
                    jnp.concatenate([group[e][v][AVG * s : AVG * s + AVG] for v in range(2)], axis=0)
                    for e in range(2)
                ]
                re = jnp.where(low, even, pltpu.roll(odd, LANES // 2, 1))
                im = jnp.where(low, pltpu.roll(even, LANES // 2, 1), odd)
                rows_k[which, base : base + 2 * AVG, lanes] = re.astype(jnp.bfloat16)
                rows_k[which, half + base : half + base + 2 * AVG, lanes] = im.astype(jnp.bfloat16)
                base += 2 * AVG
        turned = rows_k[which, :, lanes].T
        rows_i[which, lanes, :depth] = turned
        rows_i[which, lanes, depth:] = -turned[:, :half]

    @pl.when(jnp.logical_and(slot == 0, block == 0))
    def _():
        if fetch is not None:
            for copy in fetch:
                copy.start()
        lax.fori_loop(0, width // LANES, lambda q, carry: (arrange(0, q), carry)[1], 0)

    if fetch is not None:
        for which in range(CAP):
            pl.when(jnp.logical_and(slot == which, block == 0))(fetch[which].wait)

    def strip(which, i):
        upper = lax.broadcasted_iota(jnp.int32, (tile, tile), 0) <= lax.broadcasted_iota(
            jnp.int32, (tile, tile), 1
        )
        keep = valid_ref[which] != 0
        rows = slice(i * tile, (i + 1) * tile)
        for j in range(blocks):
            lanes = slice(j * tile, (j + 1) * tile)
            other = rows_k[which, :, lanes]
            real = imag = None
            if i <= j:
                real = jnp.dot(rows_i[which, rows, :depth], other, preferred_element_type=jnp.float32)
            if i >= j:
                imag = jnp.dot(rows_i[which, rows, half:], other, preferred_element_type=jnp.float32)
            value = real if imag is None else imag if real is None else jnp.where(upper, real, imag)
            if partial is not None:
                value = value + partial[which, rows, lanes].astype(jnp.float32)
            value = jnp.where(keep, value * scale, 0.0)
            if held:
                out[which, rows, lanes] = value.astype(out.dtype)
            else:
                out[0, :, lanes] = value

    each = width // LANES // blocks
    for which in range(CAP):
        for i in range(blocks):

            @pl.when(jnp.logical_and(slot == which, block == i))
            def _():
                if which + 1 < CAP:
                    for q in range(each):
                        arrange(which + 1, i * each + q)
                strip(which, i)


def correlate_call(n_inp, n_tim, mixed, scale, valid, piece, partial=None):
    width = n_inp * LANES // 2
    depth = n_tim * piece.shape[2] * 2
    tile = TILE
    block = pl.BlockSpec((1, tile, width), lambda s, i, *_: (s, i, 0))
    held = pl.BlockSpec(memory_space=pltpu.VMEM)
    more = [] if partial is None else [partial]
    return pl.pallas_call(
        functools.partial(correlate_kernel, n_tim, mixed, scale),
        out_shape=jax.ShapeDtypeStruct((CAP, width, width), jnp.float32 if more else jnp.bfloat16),
        grid_spec=pltpu.PrefetchScalarGridSpec(
            num_scalar_prefetch=1,
            grid=(CAP, width // tile),
            in_specs=[held] + [pl.BlockSpec(memory_space=pl.ANY)] * len(more),
            out_specs=block if more else held,
            scratch_shapes=[
                pltpu.VMEM((CAP, depth, width), jnp.bfloat16),
                pltpu.VMEM((CAP, width, depth + depth // 2), jnp.bfloat16),
            ]
            + [pltpu.VMEM(p.shape, p.dtype) for p in more]
            + [pltpu.SemaphoreType.DMA((CAP,)) for _ in more],
        ),
        compiler_params=pltpu.CompilerParams(vmem_limit_bytes=CORRELATE_VMEM),
        cost_estimate=pl.CostEstimate(flops=5 * 10**9, bytes_accessed=19 * 2**20, transcendentals=0),
        name="correlate",
    )(valid, piece, *more)


def body(voltages, scale_exps, owner_table):
    n_inp = lax.axis_size("inp")
    n_tim = lax.axis_size("tim")
    devices = n_inp * n_tim
    spec_dev = voltages.shape[2] // F
    *own, low2, high1 = sample_call(voltages, scale_exps)
    ahead = [(source, source + 1) for source in range(n_tim - 1)]
    back = [(source, (source - 1) % n_tim) for source in range(n_tim)]
    half = voltages.shape[1] // 2
    minus1 = lax.ppermute(own[3], "tim", ahead)
    plus0 = lax.ppermute(own[0], "tim", back)
    minus2 = lax.ppermute(low2, "tim", ahead)
    plus1 = lax.ppermute(high1, "tim", back)

    rows = owner_rows(owner_table, CAP)
    match = rows[None, :] == jnp.arange(devices * CAP, dtype=jnp.int32)[:, None]
    valid = jnp.any(match, axis=1).astype(jnp.int32)
    which = jnp.sum(jnp.where(match, jnp.arange(CH, dtype=jnp.int32)[None, :], 0), axis=1)
    first = (which * AVG - AVG * CH // 2) % F
    me = lax.axis_index("inp") * n_tim + lax.axis_index("tim")
    mine = lax.dynamic_slice(valid, (me * CAP,), (CAP,))

    table = jnp.asarray(radix_table()).astype(jnp.bfloat16)

    last = (lax.axis_index("tim") == n_tim - 1).astype(jnp.int32)
    first = jnp.concatenate([first, last[None]])
    tables = (jnp.asarray(row_table()), table)
    x0, x1, x2, x3 = [(s, 0) for s in range(spec_dev)]
    third = channel_call([[((x0, x1, x2, x3), 0)]], first, own, *tables)
    near = channel_call([[(((3, 0), x0, x1, x2), 0)]], first, (*own[:3], minus1), *tables, prior=(third,))
    near, plus0, minus2, plus1 = lax.optimization_barrier((near, plus0, minus2, plus1))
    near = lax.all_to_all(near, ("inp", "tim"), split_axis=0, concat_axis=0, tiled=True)
    m1, m2, p0, p1 = (4, 0), (5, 0), (6, 0), (7, half)
    plan = [[((x1, x2, x3, p0), 3)], [((m2, m1, x0, x1), 0), ((x2, x3, p0, p1), 2)]]
    far = channel_call(plan, first, (*own, minus1, minus2, plus0, plus1), *tables)
    far = lax.all_to_all(far, ("inp", "tim"), split_axis=0, concat_axis=0, tiled=True)
    partial = correlate_call(n_inp, n_tim, False, 1.0, mine, near)
    return correlate_call(n_inp, n_tim, True, 1.0 / (n_tim * spec_dev * AVG), mine, far, partial)


def solution(mesh):
    return jax.shard_map(
        body,
        mesh=mesh,
        in_specs=(P(None, "inp", "tim"), P("inp", "tim"), P()),
        out_specs=P(("inp", "tim"), None, None),
        check_vma=False,
    )
```

```python
import functools
import math

import jax
import jax.numpy as jnp
import numpy as np
from jax import lax
from jax.experimental import pallas as pl
from jax.experimental.pallas import tpu as pltpu
from jax.sharding import PartitionSpec as P

F = 4096
AVG = 24
CH = 144
TAPS = 4
CAP = 2
R1 = 16
R2 = 256
LANES = 128
CHANNEL_VMEM = 30 * 2**20
CORRELATE_VMEM = 50 * 2**20
TILE = 256


def row_table():
    length = TAPS * F
    steps = np.arange(length, dtype=np.float64)
    centre = (steps + 0.5 - length / 2.0) / F
    taper = 0.5 - 0.5 * np.cos(2.0 * math.pi * (steps + 0.5) / length)
    taps = (np.sinc(centre) * taper).reshape(TAPS, F)
    angle = 2.0 * math.pi * (np.arange(R1)[:, None] * np.arange(R2)[None, :]).reshape(1, F) / F
    rows = [taps, np.cos(angle) / math.sqrt(F), np.sin(angle) / math.sqrt(F), np.zeros((2, F))]
    return np.concatenate(rows, axis=0).astype(np.float32)


def radix_table():
    phase = np.arange(R2)[:, None] * np.arange(R2)[None, :] % R2
    angle = 2.0 * math.pi * phase / R2
    cosine, sine = np.cos(angle), np.sin(angle)
    table = np.concatenate(
        [np.concatenate([cosine, sine], axis=1), np.concatenate([-sine, cosine], axis=1)], axis=0
    )
    return table.astype(np.float32)


def owner_rows(owner_table, cap):
    index = jnp.arange(owner_table.shape[0], dtype=jnp.int32)
    same = owner_table[:, None] == owner_table[None, :]
    earlier = index[None, :] < index[:, None]
    slot = jnp.sum((same & earlier).astype(jnp.int32), axis=1)
    return owner_table * cap + slot


def four(a, b, c, d):
    sr, si = a[0] + c[0], a[1] + c[1]
    tr, ti = a[0] - c[0], a[1] - c[1]
    ur, ui = b[0] + d[0], b[1] + d[1]
    vr, vi = b[0] - d[0], b[1] - d[1]
    return (sr + ur, si + ui), (tr + vi, ti - vr), (sr - ur, si - ui), (tr - vi, ti + vr)


def turn(value, power):
    re, im = value
    power %= 16
    if power == 0:
        return value
    if power == 4:
        return im, -re
    root = math.sqrt(0.5)
    if power == 2:
        return (re + im) * root, (im - re) * root
    if power == 6:
        return (im - re) * root, (re + im) * (-root)
    cosine, sine = math.cos(2 * math.pi * power / 16), math.sin(2 * math.pi * power / 16)
    return re * cosine + im * sine, im * cosine - re * sine


def sixteen(x):
    inner = [four(x[b], x[4 + b], x[8 + b], x[12 + b]) for b in range(4)]
    out = [None] * 16
    for c in range(4):
        row = four(*[turn(inner[b][c], b * c) for b in range(4)])
        for d in range(4):
            out[c + 4 * d] = row[d]
    return out


def channel_kernel(plan, count, first_ref, *refs):
    xs, (rows_table, table) = refs[:count], refs[count : count + 2]
    prior, (out, turned, spectrum) = refs[count + 2 : -3], refs[-3:]
    step = pl.program_id(0)
    spectra = len(plan)
    block = 16
    inputs = turned.shape[1] // spectra
    slots = out.shape[0] * out.shape[1]
    wrapped = first_ref[slots] != 0

    def columns(s, blocks, cut, half):
        base = half * LANES
        lanes2 = pl.ds(pl.multiple_of(base, LANES), LANES)
        lanes3 = pl.ds(pl.multiple_of(base + R2, LANES), LANES)
        for r in range(block // 8):
            series = []
            for n in range(R1):
                lanes = pl.ds(pl.multiple_of(base + n * R2, LANES), LANES)
                parts = []
                for c in range(2):
                    total = None
                    for tap in range(TAPS):
                        index, skip = blocks[tap]
                        members = pl.ds(pl.multiple_of(step * block - skip, block), block)
                        value = xs[index][c, members, lanes].astype(jnp.float32)[8 * r : 8 * r + 8]
                        weight = rows_table[tap : tap + 1, lanes]
                        if tap < cut:
                            weight = jnp.where(wrapped, 0.0, weight)
                        term = weight * value
                        total = term if total is None else total + term
                    parts.append(total.astype(jnp.bfloat16).astype(jnp.float32))
                series.append(tuple(parts))
            result = sixteen(series)
            row = pl.ds(pl.multiple_of(step * block + s * inputs + 8 * r, 8), 8)
            for m in range(R1):
                re, im = result[m]
                lanes = pl.ds(pl.multiple_of(base + m * R2, LANES), LANES)
                cosine, sine = [rows_table[TAPS + k : TAPS + 1 + k, lanes] for k in range(2)]
                turned[m, row, lanes2] = re * cosine + im * sine
                turned[m, row, lanes3] = im * cosine - re * sine

    def filtered(s, blocks, cut):
        lax.fori_loop(0, R2 // LANES, lambda half, carry: (columns(s, blocks, cut, half), carry)[1], 0)

    middle = pl.num_programs(0) // 2
    for s, options in enumerate(plan):
        if len(options) == 1:
            filtered(s, *options[0])
        else:
            pl.when(step < middle)(functools.partial(filtered, s, *options[0]))
            pl.when(step >= middle)(functools.partial(filtered, s, *options[1]))

    @pl.when(step == pl.num_programs(0) - 1)
    def _():
        weights = table[...]
        low = lax.broadcasted_iota(jnp.int32, (R2, LANES), 1) < LANES // 2
        many = 4
        for m in range(0, R1, many):
            rows = turned[m : m + many].reshape(many * spectra * inputs, 2 * R2).astype(jnp.bfloat16)
            result = lax.dot_general(
                weights, rows, (((1,), (1,)), ((), ())), preferred_element_type=jnp.float32
            )
            for tile in range(many * spectra // 2):
                lanes = slice(tile * LANES, (tile + 1) * LANES)
                re, im = result[:R2, lanes], result[R2:, lanes]
                pair = (
                    jnp.where(low, re, pltpu.roll(im, LANES // 2, 1)),
                    jnp.where(low, pltpu.roll(re, LANES // 2, 1), im),
                )
                for e in range(2):
                    more, s = divmod(2 * tile + e, spectra)
                    spectrum[s, pl.ds(m + more, R2, stride=R1), :] = pair[e]

        def place(owner, carry):
            for slot in range(CAP):
                start = pl.multiple_of(first_ref[owner * CAP + slot], 8)
                rows = [p[owner, slot].astype(jnp.float32) for p in prior]
                rows += [spectrum[s, pl.ds(start, AVG), :] for s in range(spectra)]
                rows = rows[0] if len(rows) == 1 else jnp.concatenate(rows, axis=0)
                out[owner, slot] = rows.astype(jnp.bfloat16)
            return carry

        lax.fori_loop(0, out.shape[0], place, 0, unroll=8)


def channel_call(plan, first, xs, rows_table, table, prior=()):
    owners = (first.shape[0] - 1) // CAP
    block = 16
    inputs = xs[0].shape[1]
    spectra = len(plan)
    held = pl.BlockSpec(memory_space=pltpu.VMEM)
    shape = (owners, CAP, (spectra + len(prior)) * AVG, LANES)
    return pl.pallas_call(
        functools.partial(channel_kernel, plan, len(xs)),
        out_shape=jax.ShapeDtypeStruct(shape, jnp.bfloat16),
        grid_spec=pltpu.PrefetchScalarGridSpec(
            num_scalar_prefetch=1,
            grid=(inputs // block,),
            in_specs=[held] * (len(xs) + 2 + len(prior)),
            out_specs=held,
            scratch_shapes=[
                pltpu.VMEM((R1, spectra * inputs, 2 * R2), jnp.float32),
                pltpu.VMEM((spectra, F, LANES), jnp.float32),
            ],
        ),
        compiler_params=pltpu.CompilerParams(vmem_limit_bytes=CHANNEL_VMEM),
        cost_estimate=pl.CostEstimate(flops=10**9 * spectra, bytes_accessed=8 * 2**20, transcendentals=0),
        name="channels",
    )(first, *xs, rows_table, table, *prior)


def correlate_kernel(n_tim, mixed, scale, valid_ref, piece, *refs):
    if len(refs) == 6:
        partial_hbm, out, rows_k, rows_i, partial, arrived = refs
        fetch = [pltpu.make_async_copy(partial_hbm.at[k], partial.at[k], arrived.at[k]) for k in range(CAP)]
    else:
        out, rows_k, rows_i = refs
        partial = fetch = None
    slot, block = pl.program_id(0), pl.program_id(1)
    depth, width = rows_k.shape[1], rows_k.shape[2]
    held = partial is None
    tile = TILE
    blocks = width // tile
    half = depth // 2

    def arrange(which, q):
        lane = lax.broadcasted_iota(jnp.int32, (2 * AVG, LANES), 1)
        low, lower = lane < LANES // 2, lane % (LANES // 2) < LANES // 4
        lanes = pl.ds(pl.multiple_of(q * LANES, LANES), LANES)

        base = 0
        for u in range(n_tim // 2):
            group = [
                [piece[(2 * q + e) * n_tim + 2 * u + v, which].astype(jnp.float32) for v in range(2)]
                for e in range(2)
            ]
            if mixed:
                for e in range(2):
                    for v in range(2):
                        later = (2 * u + v + 1) % n_tim
                        other = piece[(2 * q + e) * n_tim + later, which].astype(jnp.float32)[AVG:]
                        mine = group[e][v]
                        turn = jnp.where(lower[:AVG], other, mine[AVG:])
                        group[e][v] = jnp.concatenate([mine[:AVG], turn], axis=0)
            for s in range(piece.shape[2] // AVG):
                even, odd = [
                    jnp.concatenate([group[e][v][AVG * s : AVG * s + AVG] for v in range(2)], axis=0)
                    for e in range(2)
                ]
                re = jnp.where(low, even, pltpu.roll(odd, LANES // 2, 1))
                im = jnp.where(low, pltpu.roll(even, LANES // 2, 1), odd)
                rows_k[which, base : base + 2 * AVG, lanes] = re.astype(jnp.bfloat16)
                rows_k[which, half + base : half + base + 2 * AVG, lanes] = im.astype(jnp.bfloat16)
                base += 2 * AVG
        turned = rows_k[which, :, lanes].T
        rows_i[which, lanes, :depth] = turned
        rows_i[which, lanes, depth:] = -turned[:, :half]

    @pl.when(jnp.logical_and(slot == 0, block == 0))
    def _():
        if fetch is not None:
            for copy in fetch:
                copy.start()
        lax.fori_loop(0, width // LANES, lambda q, carry: (arrange(0, q), carry)[1], 0)

    if fetch is not None:
        for which in range(CAP):
            pl.when(jnp.logical_and(slot == which, block == 0))(fetch[which].wait)

    def strip(which, i):
        upper = lax.broadcasted_iota(jnp.int32, (tile, tile), 0) <= lax.broadcasted_iota(
            jnp.int32, (tile, tile), 1
        )
        keep = valid_ref[which] != 0
        rows = slice(i * tile, (i + 1) * tile)
        for j in range(blocks):
            lanes = slice(j * tile, (j + 1) * tile)
            other = rows_k[which, :, lanes]
            real = imag = None
            if i <= j:
                real = jnp.dot(rows_i[which, rows, :depth], other, preferred_element_type=jnp.float32)
            if i >= j:
                imag = jnp.dot(rows_i[which, rows, half:], other, preferred_element_type=jnp.float32)
            value = real if imag is None else imag if real is None else jnp.where(upper, real, imag)
            if partial is not None:
                value = value + partial[which, rows, lanes].astype(jnp.float32)
            value = jnp.where(keep, value * scale, 0.0)
            if held:
                out[which, rows, lanes] = value.astype(out.dtype)
            else:
                out[0, :, lanes] = value

    each = width // LANES // blocks
    for which in range(CAP):
        for i in range(blocks):

            @pl.when(jnp.logical_and(slot == which, block == i))
            def _():
                if which + 1 < CAP:
                    for q in range(each):
                        arrange(which + 1, i * each + q)
                strip(which, i)


def correlate_call(n_inp, n_tim, mixed, scale, valid, piece, partial=None):
    width = n_inp * LANES // 2
    depth = n_tim * piece.shape[2] * 2
    tile = TILE
    block = pl.BlockSpec((1, tile, width), lambda s, i, *_: (s, i, 0))
    held = pl.BlockSpec(memory_space=pltpu.VMEM)
    more = [] if partial is None else [partial]
    return pl.pallas_call(
        functools.partial(correlate_kernel, n_tim, mixed, scale),
        out_shape=jax.ShapeDtypeStruct((CAP, width, width), jnp.float32 if more else jnp.bfloat16),
        grid_spec=pltpu.PrefetchScalarGridSpec(
            num_scalar_prefetch=1,
            grid=(CAP, width // tile),
            in_specs=[held] + [pl.BlockSpec(memory_space=pl.ANY)] * len(more),
            out_specs=block if more else held,
            scratch_shapes=[
                pltpu.VMEM((CAP, depth, width), jnp.bfloat16),
                pltpu.VMEM((CAP, width, depth + depth // 2), jnp.bfloat16),
            ]
            + [pltpu.VMEM(p.shape, p.dtype) for p in more]
            + [pltpu.SemaphoreType.DMA((CAP,)) for _ in more],
        ),
        compiler_params=pltpu.CompilerParams(vmem_limit_bytes=CORRELATE_VMEM),
        cost_estimate=pl.CostEstimate(flops=5 * 10**9, bytes_accessed=19 * 2**20, transcendentals=0),
        name="correlate",
    )(valid, piece, *more)


def body(voltages, scale_exps, owner_table):
    n_inp = lax.axis_size("inp")
    n_tim = lax.axis_size("tim")
    devices = n_inp * n_tim
    spec_dev = voltages.shape[2] // F
    scale = jnp.exp2(scale_exps.astype(jnp.float32)) / 128.0
    own = [
        (voltages[:, :, s * F : (s + 1) * F].astype(jnp.float32) * scale[None, :, s : s + 1]).astype(
            jnp.bfloat16
        )
        for s in range(spec_dev)
    ]
    ahead = [(source, source + 1) for source in range(n_tim - 1)]
    back = [(source, (source - 1) % n_tim) for source in range(n_tim)]
    half = voltages.shape[1] // 2
    minus1 = lax.ppermute(own[3], "tim", ahead)
    plus0 = lax.ppermute(own[0], "tim", back)
    minus2 = lax.ppermute(own[2][:, :half], "tim", ahead)
    plus1 = lax.ppermute(own[1][:, half:], "tim", back)

    rows = owner_rows(owner_table, CAP)
    match = rows[None, :] == jnp.arange(devices * CAP, dtype=jnp.int32)[:, None]
    valid = jnp.any(match, axis=1).astype(jnp.int32)
    which = jnp.sum(jnp.where(match, jnp.arange(CH, dtype=jnp.int32)[None, :], 0), axis=1)
    first = (which * AVG - AVG * CH // 2) % F
    me = lax.axis_index("inp") * n_tim + lax.axis_index("tim")
    mine = lax.dynamic_slice(valid, (me * CAP,), (CAP,))

    table = jnp.asarray(radix_table()).astype(jnp.bfloat16)

    last = (lax.axis_index("tim") == n_tim - 1).astype(jnp.int32)
    first = jnp.concatenate([first, last[None]])
    tables = (jnp.asarray(row_table()), table)
    x0, x1, x2, x3 = [(s, 0) for s in range(spec_dev)]
    third = channel_call([[((x0, x1, x2, x3), 0)]], first, own, *tables)
    near = channel_call([[(((3, 0), x0, x1, x2), 0)]], first, (*own[:3], minus1), *tables, prior=(third,))
    near, plus0, minus2, plus1 = lax.optimization_barrier((near, plus0, minus2, plus1))
    near = lax.all_to_all(near, ("inp", "tim"), split_axis=0, concat_axis=0, tiled=True)
    m1, m2, p0, p1 = (4, 0), (5, 0), (6, 0), (7, half)
    plan = [[((x1, x2, x3, p0), 3)], [((m2, m1, x0, x1), 0), ((x2, x3, p0, p1), 2)]]
    far = channel_call(plan, first, (*own, minus1, minus2, plus0, plus1), *tables)
    far = lax.all_to_all(far, ("inp", "tim"), split_axis=0, concat_axis=0, tiled=True)
    partial = correlate_call(n_inp, n_tim, False, 1.0, mine, near)
    return correlate_call(n_inp, n_tim, True, 1.0 / (n_tim * spec_dev * AVG), mine, far, partial)


def solution(mesh):
    return jax.shard_map(
        body,
        mesh=mesh,
        in_specs=(P(None, "inp", "tim"), P("inp", "tim"), P()),
        out_specs=P(("inp", "tim"), None, None),
        check_vma=False,
    )
```
